32 devices in a mesh: fibre: 4 (over z), blk: 8 (over y, x, core).
Axes of the slice: x: 2, y: 2, z: 4, core: 2. Of those that a mesh axis runs over, the one named last changes fastest.
Arguments:
- readings: bfloat16 [131072, 1024], P(('fibre', 'blk')), as said below
- values: bfloat16 [131072], P(('fibre', 'blk')), may hold values from -6 to 6
- counts: int32 [32], P(('fibre', 'blk')), may hold values from 1 to 4096, as said below
- prior_root: float32 [1024, 1024], P(('fibre', 'blk')), as said below
- prior_info: float32 [1024], P(('fibre', 'blk')), may hold values from -6 to 6
Outputs:
- post_root: float32 [1024, 1024], P('blk')
- post_info: float32 [1024], replicated
The draws below stay inside these ranges and needn't reach their ends.
Inputs may be any that keep to these rules, and one draw needn't show every extreme that they name: `counts`: every owner has at least one live row, and in every draw some owner has all 4096 rows live. `prior_root`: upper triangular with a positive diagonal. `readings`: whitened measurement rows; nothing beyond the stated range is promised.
All inputs are finite; a program needn't handle non-finite values.
Results may differ from the reference program's by a relative error of at most 0.0003.
Values sent between devices are 32-bit elements; how exact they have to be, the bound alone decides.
No kernel may reach another device: no remote copies, remote signals or barrier semaphores. Data moves between devices by JAX's collectives and lax.ppermute only.
A program may use at most 128 MiB of HBM per device.

```python
import jax
import jax.numpy as jnp
from jax import lax

NS = 1024
CAP = 4096
OWNERS = 32


def draw_counts(key, part):
    first_key, second_key = jax.random.split(jax.random.fold_in(key, 11))
    drawn = jax.random.randint(first_key, (OWNERS,), CAP // 8, CAP + 1)
    fullest = jax.random.randint(second_key, (), 0, OWNERS)
    return jnp.where(jnp.arange(OWNERS) == fullest, CAP, drawn).astype(jnp.int32)


def draw_prior_root(key, part):
    first_key, second_key = jax.random.split(jax.random.fold_in(key, 23))
    diagonal = jax.random.uniform(first_key, (NS,), jnp.float32, 1.0, 2.0)
    spread_part = jax.random.normal(second_key, (NS, NS), jnp.float32) * (0.7 / NS ** 0.5)
    places = jnp.arange(NS)
    upper_mask = places[:, None] < places[None, :]
    return jnp.where(upper_mask, spread_part, 0.0) + jnp.diag(diagonal)


def draw_readings(key, part):
    mix_key, row_key = jax.random.split(jax.random.fold_in(key, 37))
    coupling_key, left_key, right_key = jax.random.split(mix_key, 3)
    coupling_scale = 0.6 / NS ** 0.5
    row_scale = (2.0 / (CAP * OWNERS)) ** 0.5
    mode_count = 4
    coupling = jnp.clip(jax.random.normal(coupling_key, (NS, NS), jnp.float32), -3.0, 3.0) * coupling_scale
    left_modes = jnp.clip(jax.random.normal(left_key, (mode_count, NS), jnp.float32), -4.0, 4.0) * (1.0 / NS ** 0.5)
    right_modes = jnp.clip(jax.random.normal(right_key, (mode_count, NS), jnp.float32), -4.0, 4.0) * (40.0 / NS) ** 0.5
    common = jnp.dot(left_modes.T, right_modes, precision=lax.Precision.HIGHEST)
    mixing = coupling + common + jnp.eye(NS, dtype=jnp.float32)

    def one_owner(owner):
        owner_key = jax.random.fold_in(row_key, owner)
        white_key = jax.random.fold_in(owner_key, 0)
        white = jnp.clip(jax.random.normal(white_key, (CAP, NS), jnp.float32), -6.0, 6.0)
        mixed = jnp.dot(white, mixing, precision=lax.Precision.HIGHEST) * row_scale
        return mixed.astype(jnp.bfloat16)
    blocks = lax.map(one_owner, jnp.arange(OWNERS, dtype=jnp.int32))
    return blocks.reshape(OWNERS * CAP, NS)


def steps_of(rng, extent, shards, least, high):
    def one(axis_at, parts):
        steps = jax.random.uniform(jax.random.fold_in(jax.random.fold_in(rng, 6), axis_at), (parts,), jnp.float32, least / len(shards), high / len(shards))
        return jnp.repeat(jnp.exp(steps), extent[axis_at] // parts).reshape((-1,) + (1,) * (len(extent) - axis_at - 1))

    level = one(*shards[0])
    for cut in shards[1:]:
        level = level * one(*cut)
    return level


def normal_values(rng, extent, width, limit, cuts=(), held_as=jnp.bfloat16):
    level = steps_of(rng, extent, cuts, -0.22, 0.18) if cuts else 1.0
    array = jax.random.normal(rng, extent, jnp.float32) * width * level
    return jnp.minimum(jnp.maximum(array, -limit), limit).astype(held_as)


def setup_inputs(seed: int = 0) -> dict:
    keys = jax.random.split(jax.random.key(seed), 6)
    readings = draw_readings(jax.random.fold_in(keys[5], 71), 0)
    values = normal_values(keys[1], (OWNERS * CAP,), 1.0, 6.0, ((0, 32),))
    counts = draw_counts(jax.random.fold_in(keys[5], 71), 0)
    prior_root = draw_prior_root(jax.random.fold_in(keys[5], 71), 0)
    prior_info = normal_values(keys[4], (NS,), 1.0, 6.0, ((0, 32),), jnp.float32)
    return {"readings": readings, "values": values, "counts": counts, "prior_root": prior_root, "prior_info": prior_info}


def reference(readings, values, counts, prior_root, prior_info):
    owner_rows = readings.reshape(OWNERS, CAP, NS)
    owner_vals = values.reshape(OWNERS, CAP)
    positions = jnp.arange(CAP, dtype=jnp.int32)

    def add_owner(totals, owner_item):
        row_block, val_block, count_one = owner_item
        live_mask = positions < count_one
        row_block = jnp.where(live_mask[:, None], row_block, jnp.zeros((), row_block.dtype))
        val_block = jnp.where(live_mask, val_block, jnp.zeros((), val_block.dtype))
        gram_part = lax.dot_general(row_block.astype(jnp.float32), row_block.astype(jnp.float32), (((0,), (0,)), ((), ())), preferred_element_type=jnp.float32)
        info_part = jnp.dot(val_block.astype(jnp.float32), row_block.astype(jnp.float32), preferred_element_type=jnp.float32)
        return ((totals[0] + gram_part, totals[1] + info_part), None)
    initial = (jnp.zeros((NS, NS), jnp.float32), jnp.zeros((NS,), jnp.float32))
    totals, unused_out = lax.scan(add_owner, initial, (owner_rows, owner_vals, counts))
    gram_sum = totals[0] + jnp.dot(prior_root.T, prior_root, precision=lax.Precision.HIGHEST)
    info_sum = totals[1] + jnp.dot(prior_info, prior_root, precision=lax.Precision.HIGHEST)
    factor = jnp.linalg.cholesky(gram_sum)
    post_info = lax.linalg.triangular_solve(factor, info_sum[:, None], left_side=True, lower=True)[:, 0]
    return (factor.T, post_info)
```

```python
import functools

import jax
import jax.numpy as jnp
from jax import lax
from jax.experimental import pallas as pl
from jax.experimental.pallas import tpu as pltpu
from jax.sharding import PartitionSpec as P

F32 = jnp.float32
BF16 = jnp.bfloat16
NB = 128
VMEM = pltpu.CompilerParams(vmem_limit_bytes=56 * 2**20)


def split(x):
    hi = x.astype(BF16)
    return hi, (x - hi.astype(F32)).astype(BF16)


def block_at(width):
    nb = width // NB
    places, at = {}, 0
    for i in range(nb):
        for j in range(i, nb):
            places[i, j] = at
            at += 1
    return places


def dot_t(a, b):
    return lax.dot_general(a, b, (((0,), (0,)), ((), ())), preferred_element_type=F32)


def gram_kernel(step_rows, half, at_ref, rows_ref, vals_ref, prior_ref, pinfo_ref, keep_ref, send_ref, acc, info):
    t = pl.program_id(0)
    width = rows_ref.shape[1]
    tile = min(256, width)
    live = at_ref[0] - t * step_rows

    @pl.when(t == 0)
    def _():
        p = prior_ref[...]
        hi = p.astype(BF16)
        rest = p - hi.astype(F32)
        mid = rest.astype(BF16)
        lo = (rest - mid.astype(F32)).astype(BF16)
        left = jnp.concatenate([hi, hi, mid, mid, hi, lo], axis=0)
        right = jnp.concatenate([hi, mid, hi, mid, lo, hi], axis=0)
        for i in range(0, width, tile):
            acc[i : i + tile, i:] = dot_t(left[:, i : i + tile], right[:, i:])
        info[...] = jnp.broadcast_to(
            jnp.dot(pinfo_ref[...], p, precision=lax.Precision.HIGHEST, preferred_element_type=F32), info.shape
        )

    @pl.when(live > 0)
    def _():
        place = lax.broadcasted_iota(jnp.int32, (step_rows, 1), 0)
        x = jnp.where(place < live, rows_ref[...], jnp.zeros((), BF16))
        for i in range(0, width, tile):
            acc[i : i + tile, i:] += dot_t(x[:, i : i + tile], x[:, i:])
        v = jnp.broadcast_to(vals_ref[pl.ds(t, 1), :], (8, step_rows)).astype(BF16)
        info[...] += jnp.dot(v, x, preferred_element_type=F32)

    @pl.when(t == pl.num_programs(0) - 1)
    def _():
        nb = width // NB
        total = nb * (nb + 1) // 2 * NB

        def pack(halves):
            for (i, j), at in block_at(width).items():
                out, off = halves[at * NB // half], at * NB % half
                out[off : off + NB, :] = acc[i * NB : (i + 1) * NB, j * NB : (j + 1) * NB]
            out, off = halves[(total - NB) // half], (total - NB) % half + NB // 2
            hw = NB // 2
            for b in range(2 * nb):
                out[off + b : off + b + 1, 0:hw] = info[0:1, b * hw : (b + 1) * hw]
            for at in range(total, 2 * half, NB):
                halves[at // half][at % half : at % half + NB, :] = jnp.zeros((NB, NB), F32)

        @pl.when(at_ref[1] == 0)
        def _():
            pack((keep_ref, send_ref))

        @pl.when(at_ref[1] != 0)
        def _():
            pack((send_ref, keep_ref))


def gram(readings, values, counts, prior_root, prior_info, side, half):
    cap, width = readings.shape
    step_rows = min(512, cap)
    steps = cap // step_rows
    scalars = jnp.stack([counts[0], side]).astype(jnp.int32)
    whole = pl.BlockSpec(memory_space=pltpu.VMEM)
    return pl.pallas_call(
        functools.partial(gram_kernel, step_rows, half),
        grid=(steps,),
        in_specs=[
            pl.BlockSpec(memory_space=pltpu.SMEM),
            pl.BlockSpec((step_rows, width), lambda t: (t, 0)),
            whole,
            whole,
            whole,
        ],
        out_specs=[whole, whole],
        out_shape=[jax.ShapeDtypeStruct((half, NB), F32)] * 2,
        scratch_shapes=[pltpu.VMEM((width, width), F32), pltpu.VMEM((8, width), F32)],
        compiler_params=VMEM,
        name="gram",
    )(scalars, readings, values.astype(F32).reshape(steps, step_rows), prior_root, prior_info.reshape(1, -1))


def lane_of(v, at):
    return jnp.broadcast_to(v[:, at : at + 1], v.shape)


def row_of(v, at):
    return jnp.broadcast_to(v[at : at + 1, :], v.shape)


def factor_block(a):
    a = list(a)
    n = len(a)
    lane = lax.broadcasted_iota(jnp.int32, (8, NB), 1)
    sub = lax.broadcasted_iota(jnp.int32, (8, NB), 0)
    pivots = []
    for g in range(n):
        c0 = 8 * g
        col = {i: [lane_of(a[i], c0 + k) for k in range(8)] for i in range(g, n)}
        p = {(u, v): row_of(col[g][v], u) for u in range(8) for v in range(u, 8)}
        inv = [None] * 8
        for k in range(8):
            inv[k] = 1.0 / p[k, k]
            for u in range(k + 1, 8):
                f = p[k, u] * inv[k]
                for v in range(u, 8):
                    p[u, v] = p[u, v] - f * p[k, v]
        pivot = p[0, 0]
        for k in range(1, 8):
            pivot = jnp.where(sub == k, p[k, k], pivot)
        pivots.append(pivot)
        mult = {}
        for i in range(g, n):
            c = col[i]
            for k in range(8):
                m = c[k] * inv[k]
                if i == g:
                    m = jnp.where(sub > k, m, 0.0)
                mult[i, k] = m
                for v in range(k + 1, 8):
                    c[v] = c[v] - m * p[k, v]
        w = a[g]
        rows = []
        inside = (lane >= c0) & (lane < c0 + 8)
        for k in range(8):
            row = row_of(w, k)
            one = lane == c0 + k
            rows.append(jnp.where(inside & (lane > c0 + k), 0.0, jnp.where(one, 1.0, row)))
            if k < 7:
                w = jnp.where(one & (sub > k), 0.0, w) - mult[g, k] * jnp.where(one, 1.0, row)
        a[g] = w
        for i in range(g + 1, n):
            s = jnp.where(inside, 0.0, a[i])
            for k in range(8):
                s = s - mult[i, k] * rows[k]
            a[i] = s
    return a, pivots


def factor_kernel(pieces, at_ref, own_ref, far_ref, root_ref, info_ref, g, s, minv, r, uhi, ulo, y):
    nb = r.shape[0] // NB
    width = r.shape[1]
    place = block_at(width)
    side, quarter, layer = at_ref[0], at_ref[1], at_ref[2]
    n_quarter, n_layer, piece = pieces
    for ms in range(n_quarter):
        for mz in range(n_layer):
            for mc, ref in enumerate((own_ref, far_ref)):
                to = (((side ^ mc) * n_quarter + (quarter ^ ms)) * n_layer + (layer ^ mz)) * piece
                at = (ms * n_layer + mz) * piece
                g[pl.ds(pl.multiple_of(to, 8), piece), :] = ref[at : at + piece, :]

    last = place[nb - 1, nb - 1] * NB
    hw = NB // 2
    block = g[last : last + NB, :]
    mirror = block.T
    for b in range(nb):
        y[8 * b : 8 * b + 8, :] = jnp.broadcast_to(
            jnp.concatenate([block[hw + 2 * b : hw + 2 * b + 1, 0:hw], block[hw + 2 * b + 1 : hw + 2 * b + 2, 0:hw]], axis=1),
            (8, NB),
        )
    lane = lax.broadcasted_iota(jnp.int32, (hw, NB), 1)
    g[last + hw : last + NB, :] = jnp.where(lane < hw, mirror[hw:, :], block[hw:, :])

    s[:, 0:NB] = g[0:NB, :]
    lane = lax.broadcasted_iota(jnp.int32, (8, NB), 1)
    sub = lax.broadcasted_iota(jnp.int32, (8, NB), 0)

    def step(i, carry):
        a, pivots = factor_block([s[8 * u : 8 * u + 8, 0:NB] for u in range(NB // 8)])
        here = pl.multiple_of(i * NB, NB)
        for u in range(NB // 8):
            scale = lax.rsqrt(pivots[u])
            row = sub + 8 * u
            v = a[u] * scale
            s[8 * u : 8 * u + 8, 0:NB] = jnp.where(lane >= row, v, 0.0)
            minv[8 * u : 8 * u + 8, :] = jnp.where(lane < row, v, jnp.where(lane == row, scale, 0.0))
        for at in range(nb):
            @pl.when(i == at)
            def _():
                lo, hi = at * NB, at * NB + NB
                if at:
                    r[lo:hi, 0:lo] = jnp.zeros((NB, lo), F32)
                r[lo:hi, lo:hi] = s[:, 0:NB]
                m = minv[...]
                b = y[8 * at : 8 * at + 8, :]
                yi = lax.dot_general(
                    b, m, (((1,), (1,)), ((), ())), precision=lax.Precision.HIGHEST, preferred_element_type=F32
                )
                y[8 * at : 8 * at + 8, :] = yi
                if at + 1 < nb:
                    mh, ml = split(m)
                    rest = g_row(at, hi)
                    sh, sl = split(rest)
                    u = jnp.dot(
                        jnp.concatenate([mh, mh, ml], axis=1),
                        jnp.concatenate([sh, sl, sh], axis=0),
                        preferred_element_type=F32,
                    )
                    r[lo:hi, hi:] = u
                    uh, ul = split(u)
                    uhi[lo:hi, hi:] = uh
                    ulo[lo:hi, hi:] = ul
                    for b in range(at + 1, nb):
                        y[8 * b : 8 * b + 8, :] -= jnp.dot(
                            yi, u[:, b * NB - hi : b * NB - hi + NB],
                            precision=lax.Precision.HIGHEST, preferred_element_type=F32,
                        )
                    end = hi + NB
                    fh, fl = uhi[0:hi, hi:end], ulo[0:hi, hi:end]
                    for b in range(at + 1, nb):
                        c = slice(b * NB, b * NB + NB)
                        k = place[at + 1, b] * NB
                        t = g[k : k + NB, :] - (
                            dot_t(fh, uhi[0:hi, c]) + dot_t(fh, ulo[0:hi, c]) + dot_t(fl, uhi[0:hi, c])
                        )
                        if b == at + 1:
                            s[:, 0:NB] = t
                        else:
                            g[k : k + NB, :] = t
        return carry

    def g_row(i, start):
        return jnp.concatenate([g[place[i, j] * NB : place[i, j] * NB + NB, :] for j in range(start // NB, nb)], axis=1)

    lax.fori_loop(0, nb, step, 0)
    rows = root_ref.shape[0]
    root_ref[...] = r[pl.ds(pl.multiple_of(at_ref[3] * rows, 8), rows), :]
    for b in range(nb):
        info_ref[b : b + 1, :] = y[8 * b : 8 * b + 1, :]


def factor(own, far, scalars, pieces, width, rows):
    whole = pl.BlockSpec(memory_space=pltpu.VMEM)
    nb = width // NB
    return pl.pallas_call(
        functools.partial(factor_kernel, pieces),
        in_specs=[pl.BlockSpec(memory_space=pltpu.SMEM), whole, whole],
        out_specs=[whole, whole],
        out_shape=[jax.ShapeDtypeStruct((rows, width), F32), jax.ShapeDtypeStruct((nb, NB), F32)],
        scratch_shapes=[
            pltpu.VMEM((2 * own.shape[0], NB), F32),
            pltpu.VMEM((NB, NB), F32),
            pltpu.VMEM((NB, NB), F32),
            pltpu.VMEM((width, width), F32),
            pltpu.VMEM((width, width), BF16),
            pltpu.VMEM((width, width), BF16),
            pltpu.VMEM((8 * nb, NB), F32),
        ],
        compiler_params=VMEM,
        name="factor",
    )(scalars, own, far)


def swap(x, axis, mask):
    n = lax.axis_size(axis)
    return lax.ppermute(x, axis, [(d, d ^ mask) for d in range(n)])


def exchange_sum(parts, axis, masks, me):
    count = len(masks) + 1
    rows = parts[0].shape[0] // count

    def share(mask):
        terms = [lax.dynamic_slice_in_dim(x, (me ^ mask) * rows, rows, 0) for x in parts]
        return functools.reduce(lambda a, b: a + b, terms)

    out = [swap(share(m), axis, masks[m - 1]) for m in range(1, count)]
    return [share(0)] + out


def gather(x, axis, masks):
    return jnp.concatenate([x] + [swap(x, axis, m) for m in masks], axis=0)


def local(readings, values, counts, prior_root, prior_info):
    width = readings.shape[1]
    n_blk, n_fibre = lax.axis_size("blk"), lax.axis_size("fibre")
    blk, fibre = lax.axis_index("blk"), lax.axis_index("fibre")
    nb = width // NB
    unit = 8 * n_blk * n_fibre
    total = -(-(nb * (nb + 1) // 2 * NB) // unit) * unit
    half = total // 2
    side, quarter, layer = blk % 2, blk // 2, fibre
    quarters = [2 * m for m in range(1, n_blk // 2)]
    layers = list(range(1, n_fibre))

    keep, send = gram(readings, values, counts, prior_root, prior_info, side, half)
    parts = [keep, swap(send, "blk", 1)]
    parts = exchange_sum(parts, "blk", quarters, quarter)
    parts = exchange_sum(parts, "fibre", layers, layer)
    piece = functools.reduce(lambda a, b: a + b, parts)
    own = gather(gather(piece, "fibre", layers), "blk", quarters)
    far = swap(own, "blk", 1)
    scalars = jnp.stack([side, quarter, layer, blk]).astype(jnp.int32)
    rows = width // n_blk
    root, info = factor(own, far, scalars, (n_blk // 2, n_fibre, piece.shape[0]), width, rows)
    return root, info.reshape(width)


def solution(mesh):
    placed = (
        P(("fibre", "blk"), None),
        P(("fibre", "blk")),
        P(("fibre", "blk")),
        P(("fibre", "blk"), None),
        P(("fibre", "blk")),
    )
    return jax.shard_map(
        local, mesh=mesh, in_specs=placed, out_specs=(P("blk", None), P()), check_vma=False
    )
```

```python
import functools

import jax
import jax.numpy as jnp
from jax import lax
from jax.experimental import pallas as pl
from jax.experimental.pallas import tpu as pltpu
from jax.sharding import PartitionSpec as P

F32 = jnp.float32
BF16 = jnp.bfloat16
NB = 128
VMEM = pltpu.CompilerParams(vmem_limit_bytes=56 * 2**20)


def split(x):
    hi = x.astype(BF16)
    return hi, (x - hi.astype(F32)).astype(BF16)


def block_at(width):
    nb = width // NB
    places, at = {}, 0
    for i in range(nb):
        for j in range(i, nb):
            places[i, j] = at
            at += 1
    return places


def dot_t(a, b):
    return lax.dot_general(a, b, (((0,), (0,)), ((), ())), preferred_element_type=F32)


def gram_kernel(step_rows, half, at_ref, rows_ref, vals_ref, prior_ref, pinfo_ref, keep_ref, send_ref, acc, info):
    t = pl.program_id(0)
    width = rows_ref.shape[1]
    tile = min(256, width)
    live = at_ref[0] - t * step_rows

    @pl.when(t == 0)
    def _():
        p = prior_ref[...]
        hi = p.astype(BF16)
        rest = p - hi.astype(F32)
        mid = rest.astype(BF16)
        lo = (rest - mid.astype(F32)).astype(BF16)
        left = jnp.concatenate([hi, hi, mid, mid, hi, lo], axis=0)
        right = jnp.concatenate([hi, mid, hi, mid, lo, hi], axis=0)
        for i in range(0, width, tile):
            acc[i : i + tile, i:] = dot_t(left[:, i : i + tile], right[:, i:])
        info[...] = jnp.broadcast_to(
            jnp.dot(pinfo_ref[...], p, precision=lax.Precision.HIGHEST, preferred_element_type=F32), info.shape
        )

    @pl.when(live > 0)
    def _():
        place = lax.broadcasted_iota(jnp.int32, (step_rows, 1), 0)
        x = jnp.where(place < live, rows_ref[...], jnp.zeros((), BF16))
        for i in range(0, width, tile):
            acc[i : i + tile, i:] += dot_t(x[:, i : i + tile], x[:, i:])
        v = jnp.broadcast_to(vals_ref[pl.ds(t, 1), :], (8, step_rows)).astype(BF16)
        info[...] += jnp.dot(v, x, preferred_element_type=F32)

    @pl.when(t == pl.num_programs(0) - 1)
    def _():
        nb = width // NB
        total = nb * (nb + 1) // 2 * NB

        def pack(halves):
            for (i, j), at in block_at(width).items():
                out, off = halves[at * NB // half], at * NB % half
                out[off : off + NB, :] = acc[i * NB : (i + 1) * NB, j * NB : (j + 1) * NB]
            out, off = halves[(total - NB) // half], (total - NB) % half + NB // 2
            hw = NB // 2
            for b in range(2 * nb):
                out[off + b : off + b + 1, 0:hw] = info[0:1, b * hw : (b + 1) * hw]
            for at in range(total, 2 * half, NB):
                halves[at // half][at % half : at % half + NB, :] = jnp.zeros((NB, NB), F32)

        @pl.when(at_ref[1] == 0)
        def _():
            pack((keep_ref, send_ref))

        @pl.when(at_ref[1] != 0)
        def _():
            pack((send_ref, keep_ref))


def gram(readings, values, counts, prior_root, prior_info, side, half):
    cap, width = readings.shape
    step_rows = min(512, cap)
    steps = cap // step_rows
    scalars = jnp.stack([counts[0], side]).astype(jnp.int32)
    whole = pl.BlockSpec(memory_space=pltpu.VMEM)
    return pl.pallas_call(
        functools.partial(gram_kernel, step_rows, half),
        grid=(steps,),
        in_specs=[
            pl.BlockSpec(memory_space=pltpu.SMEM),
            pl.BlockSpec((step_rows, width), lambda t: (t, 0)),
            whole,
            whole,
            whole,
        ],
        out_specs=[whole, whole],
        out_shape=[jax.ShapeDtypeStruct((half, NB), F32)] * 2,
        scratch_shapes=[pltpu.VMEM((width, width), F32), pltpu.VMEM((8, width), F32)],
        compiler_params=VMEM,
        name="gram",
    )(scalars, readings, values.astype(F32).reshape(steps, step_rows), prior_root, prior_info.reshape(1, -1))


def lane_of(v, at):
    return jnp.broadcast_to(v[:, at : at + 1], v.shape)


def row_of(v, at):
    return jnp.broadcast_to(v[at : at + 1, :], v.shape)


PANEL, STRIP = 16, 32


def factor_block(read, write):
    lane = lax.broadcasted_iota(jnp.int32, (8, NB), 1)
    sub = lax.broadcasted_iota(jnp.int32, (8, NB), 0)
    groups = NB // 8
    per = STRIP // 8
    a = [read(u) for u in range(groups)]
    for t in range(NB // STRIP):
        s0 = STRIP * t
        w = a[per * t : per * t + per]
        pivot = [None] * per
        for panel in range(STRIP // PANEL):
            g0 = panel * (PANEL // 8)
            c0 = s0 + PANEL * panel
            col = {}
            for k in range(PANEL):
                for i in range(g0 + k // 8, per):
                    col[i, k] = lane_of(w[i], c0 + k)
            d = row_of(col[g0, 0], 0)
            inv = 1.0 / d
            for k in range(PANEL):
                gk, ks = g0 + k // 8, k % 8
                pivot[gk] = d if ks == 0 else jnp.where(sub == ks, d, pivot[gk])
                below = {v: row_of(col[g0 + v // 8, k], v % 8) for v in range(k + 1, PANEL)}
                if k + 1 < PANEL:
                    ahead = row_of(col[g0 + (k + 1) // 8, k + 1], (k + 1) % 8)
                    d_next = ahead - (below[k + 1] * below[k + 1]) * inv
                    inv_next = 1.0 / d_next
                one = lane == c0 + k
                row = jnp.where(one, 1.0, row_of(w[gk], ks))
                for i in range(gk, per):
                    m = col[i, k] * inv
                    if i == gk:
                        m = jnp.where(sub > ks, m, 0.0)
                    for v in range(k + 1, PANEL):
                        if i >= g0 + v // 8:
                            col[i, v] = col[i, v] - m * below[v]
                    gone = one & (sub > ks) if i == gk else one
                    w[i] = jnp.where(gone, 0.0, w[i]) - m * row
                if k + 1 < PANEL:
                    d, inv = d_next, inv_next
        inside = (lane >= s0) & (lane < s0 + STRIP)
        scaled = []
        for i in range(per):
            scale = lax.rsqrt(pivot[i])
            v = w[i] * scale
            row = sub + (s0 + 8 * i)
            lower = jnp.where(lane < row, v, jnp.where(lane == row, scale, 0.0))
            write(per * t + i, jnp.where(lane >= row, v, 0.0), lower)
            scaled.append(jnp.where(inside, lower, v))
        if s0 + STRIP < NB:
            hi, lo = split(jnp.concatenate(scaled, axis=0))
            off = dot_t(jnp.concatenate([hi, hi, lo], axis=0), jnp.concatenate([hi, lo, hi], axis=0))
            for i in range(per * (t + 1), groups):
                a[i] = jnp.where(inside, 0.0, a[i]) - off[8 * i : 8 * i + 8, :]


def factor_kernel(pieces, at_ref, own_ref, far_ref, root_ref, info_ref, g, s, minv, r, uhi, ulo, y):
    nb = r.shape[0] // NB
    width = r.shape[1]
    place = block_at(width)
    side, quarter, layer = at_ref[0], at_ref[1], at_ref[2]
    n_quarter, n_layer, piece = pieces
    for ms in range(n_quarter):
        for mz in range(n_layer):
            for mc, ref in enumerate((own_ref, far_ref)):
                to = (((side ^ mc) * n_quarter + (quarter ^ ms)) * n_layer + (layer ^ mz)) * piece
                at = (ms * n_layer + mz) * piece
                g[pl.ds(pl.multiple_of(to, 8), piece), :] = ref[at : at + piece, :]

    last = place[nb - 1, nb - 1] * NB
    hw = NB // 2
    block = g[last : last + NB, :]
    mirror = block.T
    for b in range(nb):
        y[8 * b : 8 * b + 8, :] = jnp.broadcast_to(
            jnp.concatenate([block[hw + 2 * b : hw + 2 * b + 1, 0:hw], block[hw + 2 * b + 1 : hw + 2 * b + 2, 0:hw]], axis=1),
            (8, NB),
        )
    lane = lax.broadcasted_iota(jnp.int32, (hw, NB), 1)
    g[last + hw : last + NB, :] = jnp.where(lane < hw, mirror[hw:, :], block[hw:, :])

    s[:, 0:NB] = g[0:NB, :]

    def step(i, carry):
        def read(u):
            return s[8 * u : 8 * u + 8, 0:NB]

        def write(u, upper, lower):
            s[8 * u : 8 * u + 8, 0:NB] = upper
            minv[8 * u : 8 * u + 8, :] = lower

        factor_block(read, write)
        for at in range(nb):
            @pl.when(i == at)
            def _():
                lo, hi = at * NB, at * NB + NB
                if at:
                    r[lo:hi, 0:lo] = jnp.zeros((NB, lo), F32)
                r[lo:hi, lo:hi] = s[:, 0:NB]
                m = minv[...]
                b = y[8 * at : 8 * at + 8, :]
                yi = lax.dot_general(
                    b, m, (((1,), (1,)), ((), ())), precision=lax.Precision.HIGHEST, preferred_element_type=F32
                )
                y[8 * at : 8 * at + 8, :] = yi
                if at + 1 < nb:
                    mh, ml = split(m)
                    rest = g_row(at, hi)
                    sh, sl = split(rest)
                    u = jnp.dot(
                        jnp.concatenate([mh, mh, ml], axis=1),
                        jnp.concatenate([sh, sl, sh], axis=0),
                        preferred_element_type=F32,
                    )
                    r[lo:hi, hi:] = u
                    uh, ul = split(u)
                    uhi[lo:hi, hi:] = uh
                    ulo[lo:hi, hi:] = ul
                    for b in range(at + 1, nb):
                        y[8 * b : 8 * b + 8, :] -= jnp.dot(
                            yi, u[:, b * NB - hi : b * NB - hi + NB],
                            precision=lax.Precision.HIGHEST, preferred_element_type=F32,
                        )
                    end = hi + NB
                    fh, fl = uhi[0:hi, hi:end], ulo[0:hi, hi:end]
                    for b in range(at + 1, nb):
                        c = slice(b * NB, b * NB + NB)
                        k = place[at + 1, b] * NB
                        t = g[k : k + NB, :] - (
                            dot_t(fh, uhi[0:hi, c]) + dot_t(fh, ulo[0:hi, c]) + dot_t(fl, uhi[0:hi, c])
                        )
                        if b == at + 1:
                            s[:, 0:NB] = t
                        else:
                            g[k : k + NB, :] = t
        return carry

    def g_row(i, start):
        return jnp.concatenate([g[place[i, j] * NB : place[i, j] * NB + NB, :] for j in range(start // NB, nb)], axis=1)

    lax.fori_loop(0, nb, step, 0)
    rows = root_ref.shape[0]
    root_ref[...] = r[pl.ds(pl.multiple_of(at_ref[3] * rows, 8), rows), :]
    for b in range(nb):
        info_ref[b : b + 1, :] = y[8 * b : 8 * b + 1, :]


def factor(own, far, scalars, pieces, width, rows):
    whole = pl.BlockSpec(memory_space=pltpu.VMEM)
    nb = width // NB
    return pl.pallas_call(
        functools.partial(factor_kernel, pieces),
        in_specs=[pl.BlockSpec(memory_space=pltpu.SMEM), whole, whole],
        out_specs=[whole, whole],
        out_shape=[jax.ShapeDtypeStruct((rows, width), F32), jax.ShapeDtypeStruct((nb, NB), F32)],
        scratch_shapes=[
            pltpu.VMEM((2 * own.shape[0], NB), F32),
            pltpu.VMEM((NB, NB), F32),
            pltpu.VMEM((NB, NB), F32),
            pltpu.VMEM((width, width), F32),
            pltpu.VMEM((width, width), BF16),
            pltpu.VMEM((width, width), BF16),
            pltpu.VMEM((8 * nb, NB), F32),
        ],
        compiler_params=VMEM,
        name="factor",
    )(scalars, own, far)


def swap(x, axis, mask):
    n = lax.axis_size(axis)
    return lax.ppermute(x, axis, [(d, d ^ mask) for d in range(n)])


def exchange_sum(parts, axis, masks, me):
    count = len(masks) + 1
    rows = parts[0].shape[0] // count

    def share(mask):
        terms = [lax.dynamic_slice_in_dim(x, (me ^ mask) * rows, rows, 0) for x in parts]
        return functools.reduce(lambda a, b: a + b, terms)

    out = [swap(share(m), axis, masks[m - 1]) for m in range(1, count)]
    return [share(0)] + out


def gather(x, axis, masks):
    return jnp.concatenate([x] + [swap(x, axis, m) for m in masks], axis=0)


def local(readings, values, counts, prior_root, prior_info):
    width = readings.shape[1]
    n_blk, n_fibre = lax.axis_size("blk"), lax.axis_size("fibre")
    blk, fibre = lax.axis_index("blk"), lax.axis_index("fibre")
    nb = width // NB
    unit = 8 * n_blk * n_fibre
    total = -(-(nb * (nb + 1) // 2 * NB) // unit) * unit
    half = total // 2
    side, quarter, layer = blk % 2, blk // 2, fibre
    quarters = [2 * m for m in range(1, n_blk // 2)]
    layers = list(range(1, n_fibre))

    keep, send = gram(readings, values, counts, prior_root, prior_info, side, half)
    parts = [keep, swap(send, "blk", 1)]
    parts = exchange_sum(parts, "blk", quarters, quarter)
    parts = exchange_sum(parts, "fibre", layers, layer)
    piece = functools.reduce(lambda a, b: a + b, parts)
    own = gather(gather(piece, "fibre", layers), "blk", quarters)
    far = swap(own, "blk", 1)
    scalars = jnp.stack([side, quarter, layer, blk]).astype(jnp.int32)
    rows = width // n_blk
    root, info = factor(own, far, scalars, (n_blk // 2, n_fibre, piece.shape[0]), width, rows)
    return root, info.reshape(width)


def solution(mesh):
    placed = (
        P(("fibre", "blk"), None),
        P(("fibre", "blk")),
        P(("fibre", "blk")),
        P(("fibre", "blk"), None),
        P(("fibre", "blk")),
    )
    return jax.shard_map(
        local, mesh=mesh, in_specs=placed, out_specs=(P("blk", None), P()), check_vma=False
    )
```

```python
import functools

import jax
import jax.numpy as jnp
from jax import lax
from jax.experimental import pallas as pl
from jax.experimental.pallas import tpu as pltpu
from jax.sharding import PartitionSpec as P

F32 = jnp.float32
BF16 = jnp.bfloat16
NB = 128
VMEM = pltpu.CompilerParams(vmem_limit_bytes=56 * 2**20)


def split(x):
    hi = x.astype(BF16)
    return hi, (x - hi.astype(F32)).astype(BF16)


def block_at(width):
    nb = width // NB
    places, at = {}, 0
    for i in range(nb):
        for j in range(i, nb):
            places[i, j] = at
            at += 1
    return places


def dot_t(a, b):
    return lax.dot_general(a, b, (((0,), (0,)), ((), ())), preferred_element_type=F32)


def chunks_of(width, devices):
    nb = width // NB
    unit = 8 * devices
    first = max(1, nb // 4)
    end = block_at(width)[first, first] if first < nb else nb * (nb + 1) // 2
    end += end % 2 if first < nb else 0
    cuts = [(0, end, 0, first), (end, nb * (nb + 1) // 2, first, nb)] if first < nb else [(0, end, 0, nb)]
    return [(lo, hi, i, j, -(-(hi - lo) * NB // unit) * unit) for lo, hi, i, j in cuts]


def gram_kernel(step_rows, chunks, count_ref, rows_ref, vals_ref, prior_ref, pinfo_ref, *refs):
    outs, (acc, info) = refs[:-2], refs[-2:]
    t = pl.program_id(0)
    width = rows_ref.shape[1]
    tile = min(256, width)
    live = count_ref[0] - t * step_rows

    @pl.when(t == 0)
    def _():
        p = prior_ref[...]
        hi = p.astype(BF16)
        rest = p - hi.astype(F32)
        mid = rest.astype(BF16)
        lo = (rest - mid.astype(F32)).astype(BF16)
        left = jnp.concatenate([hi, hi, mid, mid, hi, lo], axis=0)
        right = jnp.concatenate([hi, mid, hi, mid, lo, hi], axis=0)
        for i in range(0, width, tile):
            acc[i : i + tile, i:] = dot_t(left[:, i : i + tile], right[:, i:])
        info[...] = jnp.broadcast_to(
            jnp.dot(pinfo_ref[...], p, precision=lax.Precision.HIGHEST, preferred_element_type=F32), info.shape
        )

    @pl.when(live > 0)
    def _():
        place = lax.broadcasted_iota(jnp.int32, (step_rows, 1), 0)
        x = jnp.where(place < live, rows_ref[...], jnp.zeros((), BF16))
        for i in range(0, width, tile):
            acc[i : i + tile, i:] += dot_t(x[:, i : i + tile], x[:, i:])
        v = jnp.broadcast_to(vals_ref[pl.ds(t, 1), :], (8, step_rows)).astype(BF16)
        info[...] += jnp.dot(v, x, preferred_element_type=F32)

    @pl.when(t == pl.num_programs(0) - 1)
    def _():
        nb = width // NB
        side = lax.axis_index("blk") % 2

        def pack(side):
            for c, (b0, b1, _, _, rows) in enumerate(chunks):
                half = rows // 2
                pair = (outs[2 * c + side], outs[2 * c + 1 - side])
                for (i, j), at in block_at(width).items():
                    if b0 <= at < b1:
                        out, off = pair[(at - b0) * NB // half], (at - b0) * NB % half
                        out[off : off + NB, :] = acc[i * NB : (i + 1) * NB, j * NB : (j + 1) * NB]
                for row in range((b1 - b0) * NB, rows, NB):
                    pair[row // half][row % half : row % half + NB, :] = jnp.zeros((NB, NB), F32)
            hw = NB // 2
            out = outs[side]
            for b in range(2 * nb):
                out[hw + b : hw + b + 1, 0:hw] = info[0:1, b * hw : (b + 1) * hw]

        @pl.when(side == 0)
        def _():
            pack(0)

        @pl.when(side != 0)
        def _():
            pack(1)


def gram(readings, values, counts, prior_root, prior_info, chunks):
    cap, width = readings.shape
    step_rows = min(512, cap)
    steps = cap // step_rows
    whole = pl.BlockSpec(memory_space=pltpu.VMEM)
    shapes = [jax.ShapeDtypeStruct((c[4] // 2, NB), F32) for c in chunks for _ in range(2)]
    return pl.pallas_call(
        functools.partial(gram_kernel, step_rows, chunks),
        grid=(steps,),
        in_specs=[
            pl.BlockSpec(memory_space=pltpu.SMEM),
            pl.BlockSpec((step_rows, width), lambda t: (t, 0)),
            whole,
            whole,
            whole,
        ],
        out_specs=[whole] * len(shapes),
        out_shape=shapes,
        scratch_shapes=[pltpu.VMEM((width, width), F32), pltpu.VMEM((8, width), F32)],
        compiler_params=VMEM,
        name="gram",
    )(counts, readings, values.astype(F32).reshape(steps, step_rows), prior_root, prior_info.reshape(1, -1))


def lane_of(v, at):
    return jnp.broadcast_to(v[:, at : at + 1], v.shape)


def row_of(v, at):
    return jnp.broadcast_to(v[at : at + 1, :], v.shape)


PANEL, STRIP = 16, 32


def factor_block(read, write):
    lane = lax.broadcasted_iota(jnp.int32, (8, NB), 1)
    sub = lax.broadcasted_iota(jnp.int32, (8, NB), 0)
    groups = NB // 8
    per = STRIP // 8
    a = [read(u) for u in range(groups)]
    for t in range(NB // STRIP):
        s0 = STRIP * t
        w = a[per * t : per * t + per]
        pivot = [None] * per
        for panel in range(STRIP // PANEL):
            g0 = panel * (PANEL // 8)
            c0 = s0 + PANEL * panel
            col = {}
            for k in range(PANEL):
                for i in range(g0 + k // 8, per):
                    col[i, k] = lane_of(w[i], c0 + k)
            d = row_of(col[g0, 0], 0)
            inv = 1.0 / d
            for k in range(PANEL):
                gk, ks = g0 + k // 8, k % 8
                pivot[gk] = d if ks == 0 else jnp.where(sub == ks, d, pivot[gk])
                below = {v: row_of(col[g0 + v // 8, k], v % 8) for v in range(k + 1, PANEL)}
                if k + 1 < PANEL:
                    ahead = row_of(col[g0 + (k + 1) // 8, k + 1], (k + 1) % 8)
                    d_next = ahead - (below[k + 1] * below[k + 1]) * inv
                    inv_next = 1.0 / d_next
                one = lane == c0 + k
                row = jnp.where(one, 1.0, row_of(w[gk], ks))
                for i in range(gk, per):
                    m = col[i, k] * inv
                    if i == gk:
                        m = jnp.where(sub > ks, m, 0.0)
                    for v in range(k + 1, PANEL):
                        if i >= g0 + v // 8:
                            col[i, v] = col[i, v] - m * below[v]
                    gone = one & (sub > ks) if i == gk else one
                    w[i] = jnp.where(gone, 0.0, w[i]) - m * row
                if k + 1 < PANEL:
                    d, inv = d_next, inv_next
        inside = (lane >= s0) & (lane < s0 + STRIP)
        scaled = []
        for i in range(per):
            scale = lax.rsqrt(pivot[i])
            v = w[i] * scale
            row = sub + (s0 + 8 * i)
            lower = jnp.where(lane < row, v, jnp.where(lane == row, scale, 0.0))
            write(per * t + i, jnp.where(lane >= row, v, 0.0), lower)
            scaled.append(jnp.where(inside, lower, v))
        if s0 + STRIP < NB:
            hi, lo = split(jnp.concatenate(scaled, axis=0))
            off = dot_t(jnp.concatenate([hi, hi, lo], axis=0), jnp.concatenate([hi, lo, hi], axis=0))
            for i in range(per * (t + 1), groups):
                a[i] = jnp.where(inside, 0.0, a[i]) - off[8 * i : 8 * i + 8, :]


def factor_kernel(chunk, n_quarter, n_layer, width, *refs):
    b0, b1, first, last, sent = chunk
    nb = width // NB
    place = block_at(width)
    own_ref, far_ref, refs = refs[0], refs[1], refs[2:]
    if first:
        (hi_in, lo_in, y_in, block_in, root_in), refs = refs[:5], refs[5:]
    root_ref, y_ref, refs = refs[0], refs[1], refs[2:]
    if last < nb:
        (hi_out, lo_out, block_out), refs = refs[:3], refs[3:]
    g, s, minv, r, uhi, ulo, y = refs
    blk, layer = lax.axis_index("blk"), lax.axis_index("fibre")
    side, quarter = blk % 2, blk // 2
    piece = sent // (2 * n_quarter * n_layer)
    for ms in range(n_quarter):
        for mz in range(n_layer):
            for mc, ref in enumerate((own_ref, far_ref)):
                to = (((side ^ mc) * n_quarter + (quarter ^ ms)) * n_layer + (layer ^ mz)) * piece
                at = (ms * n_layer + mz) * piece
                g[pl.ds(pl.multiple_of(to, 8), piece), :] = ref[at : at + piece, :]

    def block(i, j):
        k = (place[i, j] - b0) * NB
        return g[k : k + NB, :] if k >= 0 else block_in[...]

    if first == 0:
        hw = NB // 2
        corner = g[0:NB, :]
        mirror = corner.T
        for b in range(nb):
            y[8 * b : 8 * b + 8, :] = jnp.broadcast_to(
                jnp.concatenate([corner[hw + 2 * b + e : hw + 2 * b + e + 1, 0:hw] for e in range(2)], axis=1), (8, NB)
            )
        lane = lax.broadcasted_iota(jnp.int32, (hw, NB), 1)
        g[hw:NB, :] = jnp.where(lane < hw, mirror[hw:, :], corner[hw:, :])
    else:
        y[...] = y_in[...]
        uhi[0 : first * NB, :] = hi_in[...]
        ulo[0 : first * NB, :] = lo_in[...]

    def next_row(at):
        lo, hi = at * NB, at * NB + NB
        if at:
            fh, fl = uhi[0:lo, lo:hi], ulo[0:lo, lo:hi]
        for b in range(at, nb):
            t = block(at, b)
            if at:
                c = slice(b * NB, b * NB + NB)
                t = t - (dot_t(fh, uhi[0:lo, c]) + dot_t(fh, ulo[0:lo, c]) + dot_t(fl, uhi[0:lo, c]))
            s[:, (b - at) * NB : (b - at) * NB + NB] = t

    next_row(first)

    def read(u):
        return s[8 * u : 8 * u + 8, 0:NB]

    def write(u, upper, lower):
        s[8 * u : 8 * u + 8, 0:NB] = upper
        minv[8 * u : 8 * u + 8, :] = lower

    def step(i, carry):
        factor_block(read, write)
        for at in range(first, last):
            @pl.when(i == at)
            def _():
                lo, hi = at * NB, at * NB + NB
                here = slice(lo - first * NB, hi - first * NB)
                if at:
                    r[here, 0:lo] = jnp.zeros((NB, lo), F32)
                r[here, lo:hi] = s[:, 0:NB]
                m = minv[...]
                yi = lax.dot_general(
                    y[8 * at : 8 * at + 8, :], m, (((1,), (1,)), ((), ())),
                    precision=lax.Precision.HIGHEST, preferred_element_type=F32,
                )
                y[8 * at : 8 * at + 8, :] = yi
                if at + 1 < nb:
                    mh, ml = split(m)
                    sh, sl = split(s[:, NB : (nb - at) * NB])
                    u = jnp.dot(
                        jnp.concatenate([mh, mh, ml], axis=1),
                        jnp.concatenate([sh, sl, sh], axis=0),
                        preferred_element_type=F32,
                    )
                    r[here, hi:] = u
                    uh, ul = split(u)
                    uhi[lo:hi, hi:] = uh
                    ulo[lo:hi, hi:] = ul
                    for b in range(at + 1, nb):
                        y[8 * b : 8 * b + 8, :] -= jnp.dot(
                            yi, u[:, b * NB - hi : b * NB - hi + NB],
                            precision=lax.Precision.HIGHEST, preferred_element_type=F32,
                        )
                    if at + 1 < last:
                        next_row(at + 1)
        return carry

    lax.fori_loop(first, last, step, 0)
    rows = root_ref.shape[0]
    start = blk * rows - first * NB
    if first:
        root_ref[...] = root_in[...]

    @pl.when((start >= 0) & (start < (last - first) * NB))
    def _():
        root_ref[...] = r[pl.ds(pl.multiple_of(start, 8), rows), :]

    if last < nb:
        y_ref[...] = y[...]
        hi_out[...] = uhi[first * NB : last * NB, :]
        lo_out[...] = ulo[first * NB : last * NB, :]
        block_out[...] = g[(place[last, last] - b0) * NB : (place[last, last] - b0 + 1) * NB, :] if b1 > place[last, last] else jnp.zeros((NB, NB), F32)
    else:
        for b in range(nb):
            y_ref[b : b + 1, :] = y[8 * b : 8 * b + 1, :]


def factor(own, far, state, chunk, n_quarter, n_layer, width, rows):
    whole = pl.BlockSpec(memory_space=pltpu.VMEM)
    nb = width // NB
    b0, b1, first, last, sent = chunk
    shapes = [jax.ShapeDtypeStruct((rows, width), F32)]
    if last < nb:
        shapes += [
            jax.ShapeDtypeStruct((8 * nb, NB), F32),
            jax.ShapeDtypeStruct((last * NB, width), BF16),
            jax.ShapeDtypeStruct((last * NB, width), BF16),
            jax.ShapeDtypeStruct((NB, NB), F32),
        ]
    else:
        shapes += [jax.ShapeDtypeStruct((nb, NB), F32)]
    args = [own, far]
    if first:
        root, y, hi, lo, block = state
        args += [hi, lo, y, block, root]
    return pl.pallas_call(
        functools.partial(factor_kernel, chunk, n_quarter, n_layer, width),
        in_specs=[whole] * len(args),
        out_specs=[whole] * len(shapes),
        out_shape=shapes,
        scratch_shapes=[
            pltpu.VMEM((sent, NB), F32),
            pltpu.VMEM((NB, width), F32),
            pltpu.VMEM((NB, NB), F32),
            pltpu.VMEM(((last - first) * NB, width), F32),
            pltpu.VMEM((width, width), BF16),
            pltpu.VMEM((width, width), BF16),
            pltpu.VMEM((8 * nb, NB), F32),
        ],
        compiler_params=VMEM,
        cost_estimate=pl.CostEstimate(flops=(last - first) * 4_000_000_000, bytes_accessed=4 * sent * NB, transcendentals=0),
        name="factor_rows_%d" % first,
    )(*args)


def swap(x, axis, mask):
    n = lax.axis_size(axis)
    return lax.ppermute(x, axis, [(d, d ^ mask) for d in range(n)])


def exchange_sum(parts, axis, masks, me):
    count = len(masks) + 1
    rows = parts[0].shape[0] // count

    def share(mask):
        terms = [lax.dynamic_slice_in_dim(x, (me ^ mask) * rows, rows, 0) for x in parts]
        return functools.reduce(lambda a, b: a + b, terms)

    out = [swap(share(m), axis, masks[m - 1]) for m in range(1, count)]
    return [share(0)] + out


def gather(x, axis, masks):
    return jnp.concatenate([x] + [swap(x, axis, m) for m in masks], axis=0)


def local(readings, values, counts, prior_root, prior_info):
    width = readings.shape[1]
    n_blk, n_fibre = lax.axis_size("blk"), lax.axis_size("fibre")
    blk, fibre = lax.axis_index("blk"), lax.axis_index("fibre")
    quarter, layer = blk // 2, fibre
    quarters = [2 * m for m in range(1, n_blk // 2)]
    layers = list(range(1, n_fibre))
    chunks = chunks_of(width, n_blk * n_fibre)

    terms = gram(readings, values, counts, prior_root, prior_info, chunks)
    state = None
    for c, chunk in enumerate(chunks):
        keep, send = terms[2 * c : 2 * c + 2]
        parts = [keep, swap(send, "blk", 1)]
        parts = exchange_sum(parts, "blk", quarters, quarter)
        parts = exchange_sum(parts, "fibre", layers, layer)
        piece = functools.reduce(lambda a, b: a + b, parts)
        own = gather(gather(piece, "fibre", layers), "blk", quarters)
        far = swap(own, "blk", 1)
        state = factor(own, far, state, chunk, n_blk // 2, n_fibre, width, width // n_blk)
    return state[0], state[1].reshape(width)


def solution(mesh):
    placed = (
        P(("fibre", "blk"), None),
        P(("fibre", "blk")),
        P(("fibre", "blk")),
        P(("fibre", "blk"), None),
        P(("fibre", "blk")),
    )
    return jax.shard_map(
        local, mesh=mesh, in_specs=placed, out_specs=(P("blk", None), P()), check_vma=False
    )
```

```python
import functools

import jax
import jax.numpy as jnp
from jax import lax
from jax.experimental import pallas as pl
from jax.experimental.pallas import tpu as pltpu
from jax.sharding import PartitionSpec as P

F32 = jnp.float32
BF16 = jnp.bfloat16
NB = 128
VMEM = pltpu.CompilerParams(vmem_limit_bytes=56 * 2**20)


def split(x):
    hi = x.astype(BF16)
    return hi, (x - hi.astype(F32)).astype(BF16)


def block_at(width):
    nb = width // NB
    places, at = {}, 0
    for i in range(nb):
        for j in range(i, nb):
            places[i, j] = at
            at += 1
    return places


def dot_t(a, b):
    return lax.dot_general(a, b, (((0,), (0,)), ((), ())), preferred_element_type=F32)


def gram_kernel(step_rows, sent, count_ref, rows_ref, vals_ref, prior_ref, pinfo_ref, keep_ref, send_ref, acc, info):
    t = pl.program_id(0)
    width = rows_ref.shape[1]
    nb = width // NB
    live = count_ref[0] - t * step_rows
    tile = min(2 * NB, width)
    tiles = [(i, i + tile, i, width) for i in range(0, width, tile)]

    @pl.when(t == 0)
    def _():
        p = prior_ref[...]
        hi = p.astype(BF16)
        rest = p - hi.astype(F32)
        mid = rest.astype(BF16)
        lo = (rest - mid.astype(F32)).astype(BF16)
        left = jnp.concatenate([hi, hi, mid, mid, hi, lo], axis=0)
        right = jnp.concatenate([hi, mid, hi, mid, lo, hi], axis=0)
        for i0, i1, j0, j1 in tiles:
            acc[i0:i1, j0:j1] = dot_t(left[:, i0:i1], right[:, j0:j1])
        info[...] = jnp.broadcast_to(
            jnp.dot(pinfo_ref[...], p, precision=lax.Precision.HIGHEST, preferred_element_type=F32), info.shape
        )

    @pl.when(live > 0)
    def _():
        place = lax.broadcasted_iota(jnp.int32, (step_rows, 1), 0)
        x = jnp.where(place < live, rows_ref[...], jnp.zeros((), BF16))
        for i0, i1, j0, j1 in tiles:
            acc[i0:i1, j0:j1] += dot_t(x[:, i0:i1], x[:, j0:j1])
        v = vals_ref[pl.ds(pl.multiple_of(t * step_rows, step_rows), step_rows)].astype(F32).reshape(1, step_rows)
        v = jnp.broadcast_to(v, (8, step_rows)).astype(BF16)
        info[...] += jnp.dot(v, x, preferred_element_type=F32)

    @pl.when(t == pl.num_programs(0) - 1)
    def _():
        half = sent // 2
        side = lax.axis_index("blk") % 2

        def pack(pair):
            for (i, j), n in block_at(width).items():
                out, off = pair[n * NB // half], n * NB % half
                out[off : off + NB, :] = acc[i * NB : (i + 1) * NB, j * NB : (j + 1) * NB]
            for row in range(nb * (nb + 1) // 2 * NB, sent, NB):
                pair[row // half][row % half : row % half + NB, :] = jnp.zeros((NB, NB), F32)
            hw = NB // 2
            for b in range(2 * nb):
                pair[0][hw + b : hw + b + 1, 0:hw] = info[0:1, b * hw : (b + 1) * hw]

        @pl.when(side == 0)
        def _():
            pack((keep_ref, send_ref))

        @pl.when(side != 0)
        def _():
            pack((send_ref, keep_ref))


def gram(readings, values, counts, prior_root, prior_info, sent):
    cap, width = readings.shape
    step_rows = min(1024, cap)
    whole = pl.BlockSpec(memory_space=pltpu.VMEM)
    return pl.pallas_call(
        functools.partial(gram_kernel, step_rows, sent),
        grid=(cap // step_rows,),
        in_specs=[
            pl.BlockSpec(memory_space=pltpu.SMEM),
            pl.BlockSpec((step_rows, width), lambda t: (t, 0)),
            whole,
            whole,
            whole,
        ],
        out_specs=[whole] * 2,
        out_shape=[jax.ShapeDtypeStruct((sent // 2, NB), F32)] * 2,
        scratch_shapes=[pltpu.VMEM((width, width), F32), pltpu.VMEM((8, width), F32)],
        compiler_params=VMEM,
        cost_estimate=pl.CostEstimate(flops=2 * cap * width * width, bytes_accessed=2 * cap * width, transcendentals=0),
        name="gram",
    )(counts, readings, values, prior_root, prior_info.reshape(1, -1))


def lane_of(v, at):
    return jnp.broadcast_to(v[:, at : at + 1], v.shape)


def row_of(v, at):
    return jnp.broadcast_to(v[at : at + 1, :], v.shape)


PANEL, STRIP = 16, 32


def factor_block(read, write, other_work):
    lane = lax.broadcasted_iota(jnp.int32, (8, NB), 1)
    sub = lax.broadcasted_iota(jnp.int32, (8, NB), 0)
    groups = NB // 8
    per = STRIP // 8
    a = [read(u) for u in range(groups)]
    for t in range(NB // STRIP):
        s0 = STRIP * t
        w = a[per * t : per * t + per]
        pivot = [None] * per
        for panel in range(STRIP // PANEL):
            g0 = panel * (PANEL // 8)
            c0 = s0 + PANEL * panel
            col = {}
            for k in range(PANEL):
                for i in range(g0 + k // 8, per):
                    col[i, k] = lane_of(w[i], c0 + k)
            next(other_work, None)
            d = row_of(col[g0, 0], 0)
            inv = 1.0 / d
            for k in range(PANEL):
                gk, ks = g0 + k // 8, k % 8
                pivot[gk] = d if ks == 0 else jnp.where(sub == ks, d, pivot[gk])
                below = {v: row_of(col[g0 + v // 8, k], v % 8) for v in range(k + 1, PANEL)}
                if k + 1 < PANEL:
                    ahead = row_of(col[g0 + (k + 1) // 8, k + 1], (k + 1) % 8)
                    d_next = ahead - (below[k + 1] * below[k + 1]) * inv
                    inv_next = 1.0 / d_next
                one = lane == c0 + k
                row = jnp.where(one, 1.0, row_of(w[gk], ks))
                for i in range(gk, per):
                    m = col[i, k] * inv
                    if i == gk:
                        m = jnp.where(sub > ks, m, 0.0)
                    for v in range(k + 1, PANEL):
                        if i >= g0 + v // 8:
                            col[i, v] = col[i, v] - m * below[v]
                    gone = one & (sub > ks) if i == gk else one
                    w[i] = jnp.where(gone, 0.0, w[i]) - m * row
                if k + 1 < PANEL:
                    d, inv = d_next, inv_next
        inside = (lane >= s0) & (lane < s0 + STRIP)
        scaled = []
        for i in range(per):
            scale = lax.rsqrt(pivot[i])
            v = w[i] * scale
            row = sub + (s0 + 8 * i)
            lower = jnp.where(lane < row, v, jnp.where(lane == row, scale, 0.0))
            write(per * t + i, jnp.where(lane >= row, v, 0.0), lower)
            scaled.append(jnp.where(inside, lower, v))
        if s0 + STRIP < NB:
            hi, lo = split(jnp.concatenate(scaled, axis=0))
            off = dot_t(jnp.concatenate([hi, hi, lo], axis=0), jnp.concatenate([hi, lo, hi], axis=0))
            for i in range(per * (t + 1), groups):
                a[i] = jnp.where(inside, 0.0, a[i]) - off[8 * i : 8 * i + 8, :]


def three(hi, lo, axis):
    return jnp.concatenate([hi, hi, lo], axis=axis)


def three_other(hi, lo, axis):
    return jnp.concatenate([hi, lo, hi], axis=axis)


def factor_kernel(n_quarter, n_layer, own_ref, far_ref, root_ref, info_ref, g, s, minv, r, uhi, ulo, thi, tlo, y):
    width = r.shape[1]
    nb = width // NB
    place = block_at(width)
    blk, layer = lax.axis_index("blk"), lax.axis_index("fibre")
    side, quarter = blk % 2, blk // 2
    piece = own_ref.shape[0] // (n_quarter * n_layer)
    for ms in range(n_quarter):
        for mz in range(n_layer):
            for mc, ref in enumerate((own_ref, far_ref)):
                to = (((side ^ mc) * n_quarter + (quarter ^ ms)) * n_layer + (layer ^ mz)) * piece
                at = (ms * n_layer + mz) * piece
                g[pl.ds(pl.multiple_of(to, 8), piece), :] = ref[at : at + piece, :]

    def block(i, j):
        return g[place[i, j] * NB : place[i, j] * NB + NB, :]

    def span(i):
        return slice(i * NB, i * NB + NB)

    hw = NB // 2
    corner = g[0:NB, :]
    mirror = corner.T
    for b in range(2 * nb):
        y[:, b * hw : (b + 1) * hw] = jnp.broadcast_to(corner[hw + b : hw + b + 1, 0:hw], (8, hw))
    lane = lax.broadcasted_iota(jnp.int32, (hw, NB), 1)
    s[0:hw, 0:NB] = corner[0:hw, :]
    s[hw:NB, 0:NB] = jnp.where(lane < hw, mirror[hw:, :], corner[hw:, :])
    for b in range(1, nb):
        s[0:NB, span(b)] = block(0, b)

    def inverse(i):
        return split(minv[span(i), :])

    def solve(i, c):
        mh, ml = inverse(i)
        sh, sl = split(s[span(i), c])
        u = jnp.dot(three(mh, ml, 1), three_other(sh, sl, 0), preferred_element_type=F32)
        r[span(i), c] = u
        uh, ul = split(u)
        uhi[span(i), c] = uh
        ulo[span(i), c] = ul
        for b in range(c.start // NB, c.stop // NB):
            t = u[:, b * NB - c.start : b * NB - c.start + NB].T
            th, tl = split(t)
            thi[span(b), span(i)] = th
            tlo[span(b), span(i)] = tl

    def reduce(i, c):
        up = slice(0, i * NB)
        off = jnp.dot(
            three(thi[span(i), up], tlo[span(i), up], 1),
            three_other(uhi[up, c], ulo[up, c], 0),
            preferred_element_type=F32,
        )
        for b in range(c.start // NB, c.stop // NB):
            s[span(i), span(b)] = block(i, b) - off[:, b * NB - c.start : b * NB - c.start + NB]

    def rest_of(i):
        cuts = [slice(c, min(c + 2 * NB, width)) for c in range((i + 2) * NB, width, 2 * NB)]
        for c in cuts:
            solve(i, c)
            yield
        for c in cuts:
            reduce(i + 1, c)
            yield
        mh, ml = inverse(i)
        bh, bl = split(y[:, span(i)])
        yi = lax.dot_general(
            three(bh, bl, 1), three_other(mh, ml, 1), (((1,), (1,)), ((), ())), preferred_element_type=F32
        )
        y[:, span(i)] = yi
        yield
        if i + 1 < nb:
            c = slice((i + 1) * NB, width)
            yh, yl = split(yi)
            y[:, c] -= jnp.dot(
                three(yh, yl, 1), three_other(uhi[span(i), c], ulo[span(i), c], 0), preferred_element_type=F32
            )
            yield
        if i:
            r[span(i), 0 : i * NB] = jnp.zeros((NB, i * NB), F32)
            yield

    other_work = iter(())
    for i in range(nb):

        def read(u):
            return s[i * NB + 8 * u : i * NB + 8 * u + 8, span(i)]

        def write(u, upper, lower):
            at = slice(i * NB + 8 * u, i * NB + 8 * u + 8)
            r[at, span(i)] = upper
            minv[at, :] = lower

        factor_block(read, write, other_work)
        for _ in other_work:
            pass
        if i + 1 < nb:
            solve(i, span(i + 1))
            reduce(i + 1, span(i + 1))
        other_work = rest_of(i)
    for _ in other_work:
        pass
    rows = root_ref.shape[0]
    root_ref[...] = r[pl.ds(pl.multiple_of(blk * rows, 8), rows), :]
    for b in range(nb):
        info_ref[b : b + 1, :] = y[0:1, span(b)]


def factor(own, far, n_quarter, n_layer, width, rows):
    whole = pl.BlockSpec(memory_space=pltpu.VMEM)
    nb = width // NB
    return pl.pallas_call(
        functools.partial(factor_kernel, n_quarter, n_layer),
        in_specs=[whole] * 2,
        out_specs=[whole] * 2,
        out_shape=[jax.ShapeDtypeStruct((rows, width), F32), jax.ShapeDtypeStruct((nb, NB), F32)],
        scratch_shapes=[
            pltpu.VMEM((2 * own.shape[0], NB), F32),
            pltpu.VMEM((width, width), F32),
            pltpu.VMEM((width, NB), F32),
            pltpu.VMEM((width, width), F32),
        ]
        + [pltpu.VMEM((width, width), BF16)] * 4
        + [pltpu.VMEM((8, width), F32)],
        compiler_params=VMEM,
        name="factor",
    )(own, far)


def swap(x, axis, mask):
    n = lax.axis_size(axis)
    return lax.ppermute(x, axis, [(d, d ^ mask) for d in range(n)])


def shares(parts, count, me):
    rows = parts[0].shape[0] // count
    return [
        functools.reduce(lambda a, b: a + b, [lax.dynamic_slice_in_dim(x, (me ^ m) * rows, rows, 0) for x in parts])
        for m in range(count)
    ]


def trade(mine, axis, masks):
    return [mine[0]] + [swap(x, axis, m) for x, m in zip(mine[1:], masks)]


def gather(x, axis, masks):
    return jnp.concatenate([x] + [swap(x, axis, m) for m in masks], axis=0)


def local(readings, values, counts, prior_root, prior_info):
    width = readings.shape[1]
    n_blk, n_fibre = lax.axis_size("blk"), lax.axis_size("fibre")
    blk, fibre = lax.axis_index("blk"), lax.axis_index("fibre")
    n_quarter = n_blk // 2
    quarters = [2 * m for m in range(1, n_quarter)]
    layers = list(range(1, n_fibre))
    unit = 8 * n_blk * n_fibre
    nb = width // NB
    sent = -(-(nb * (nb + 1) // 2 * NB) // unit) * unit

    keep, send = gram(readings, values, counts, prior_root, prior_info, sent)
    parts = [keep, swap(send, "blk", 1)]
    parts = trade(shares(parts, n_quarter, blk // 2), "blk", quarters)
    parts = trade(shares(parts, n_fibre, fibre), "fibre", layers)
    own = functools.reduce(lambda x, y: x + y, parts)
    own = gather(gather(own, "fibre", layers), "blk", quarters)
    far = swap(own, "blk", 1)
    root, info = factor(own, far, n_quarter, n_fibre, width, width // n_blk)
    return root, info.reshape(width)


def solution(mesh):
    placed = (
        P(("fibre", "blk"), None),
        P(("fibre", "blk")),
        P(("fibre", "blk")),
        P(("fibre", "blk"), None),
        P(("fibre", "blk")),
    )
    return jax.shard_map(
        local, mesh=mesh, in_specs=placed, out_specs=(P("blk", None), P()), check_vma=False
    )
```

```python
import functools

import jax
import jax.numpy as jnp
from jax import lax
from jax.experimental import pallas as pl
from jax.experimental.pallas import tpu as pltpu
from jax.sharding import PartitionSpec as P

F32 = jnp.float32
BF16 = jnp.bfloat16
NB = 128


def vmem(mib):
    return pltpu.CompilerParams(vmem_limit_bytes=mib * 2**20)


def split(x):
    hi = x.astype(BF16)
    return hi, (x - hi.astype(F32)).astype(BF16)


def block_at(width):
    nb = width // NB
    places, at = {}, 0
    for i in range(nb):
        for j in range(i, nb):
            places[i, j] = at
            at += 1
    return places


def dot_t(a, b):
    return lax.dot_general(a, b, (((0,), (0,)), ((), ())), preferred_element_type=F32)


def row_cuts(cap):
    cuts = [0, cap // 8, 3 * cap // 8, 5 * cap // 8, cap]
    return list(zip(cuts[:-1], cuts[1:])) if cap % 128 == 0 else [(0, cap)]


def gram_kernel(sent, count_ref, rows_ref, vals_ref, prior_ref, pinfo_ref, keep_ref, send_ref, x, stage, acc, info, sem, out_sem):
    cap, width = rows_ref.shape
    nb = width // NB
    half = sent // 2
    total = nb * (nb + 1) // 2 * NB
    tile = min(2 * NB, width)
    tiles = [(i, i + tile) for i in range(0, width, tile)]
    parts = row_cuts(cap)
    copies = [
        pltpu.make_async_copy(rows_ref.at[pl.ds(lo, hi - lo), :], x.at[pl.ds(lo, hi - lo), :], sem.at[n])
        for n, (lo, hi) in enumerate(parts)
    ]
    for copy in copies:
        copy.start()

    p = prior_ref[...]
    hi = p.astype(BF16)
    rest = p - hi.astype(F32)
    mid = rest.astype(BF16)
    lo = (rest - mid.astype(F32)).astype(BF16)
    left = jnp.concatenate([hi, hi, mid, mid, hi, lo], axis=0)
    right = jnp.concatenate([hi, mid, hi, mid, lo, hi], axis=0)
    for i, j in tiles:
        acc[i:j, i:] = dot_t(left[:, i:j], right[:, i:])
    info[...] = jnp.broadcast_to(
        jnp.dot(pinfo_ref[...], p, precision=lax.Precision.HIGHEST, preferred_element_type=F32), info.shape
    )
    for row in range(total, sent, NB):
        stage[row : row + NB, :] = jnp.zeros((NB, NB), F32)

    place = block_at(width)
    ends = [place[j // NB, j // NB] * NB if j < width else sent for _, j in tiles]
    cuts = sorted({0, half, *ends})
    pieces = list(zip(cuts[:-1], cuts[1:]))
    side = lax.axis_index("blk") % 2

    def out_copy(n, at_side):
        lo, hi = pieces[n]
        to = keep_ref if lo // half == at_side else send_ref
        return pltpu.make_async_copy(
            stage.at[pl.ds(lo, hi - lo), :], to.at[pl.ds(lo % half, hi - lo), :], out_sem.at[n]
        )

    def on_each_side(do):
        for at_side in range(2):
            pl.when(side == at_side)(functools.partial(do, at_side))

    sent_out = 0
    for n, (lo, hi) in enumerate(parts):
        copies[n].wait()
        live = count_ref[0] - lo

        @pl.when(live < hi - lo)
        def _():
            row = lax.broadcasted_iota(jnp.int32, (hi - lo, 1), 0)
            x[lo:hi, :] = jnp.where(row < live, x[lo:hi, :], jnp.zeros((), BF16))

        v = vals_ref[lo:hi].astype(F32).reshape(1, hi - lo)
        v = jnp.broadcast_to(v, (16, hi - lo)).astype(BF16)
        for (i, j), end in zip(tiles, ends):
            if i == 0:
                left = jnp.concatenate([x[lo:hi, i:j].T, v], axis=0)
                both = jnp.dot(left, x[lo:hi, :], preferred_element_type=F32)
                term = acc[i:j, i:] + both[0 : j - i, :]
                info[...] += both[j - i : j - i + 8, :]
            else:
                term = acc[i:j, i:] + dot_t(x[lo:hi, i:j], x[lo:hi, i:])
            if n + 1 < len(parts):
                acc[i:j, i:] = term
                continue
            for bi in range(i // NB, j // NB):
                for bj in range(bi, nb):
                    at = place[bi, bj] * NB
                    stage[at : at + NB, :] = term[bi * NB - i : bi * NB - i + NB, bj * NB - i : bj * NB - i + NB]
            if i == 0:
                hw = NB // 2
                for b in range(2 * nb):
                    stage[hw + b : hw + b + 1, 0:hw] = info[0:1, b * hw : (b + 1) * hw]
            done = [m for m, (_, stop) in enumerate(pieces) if stop <= end and m >= sent_out]
            on_each_side(lambda at_side, done=done: [out_copy(m, at_side).start() for m in done] and None)
            sent_out += len(done)
    on_each_side(lambda at_side: [out_copy(m, at_side).wait() for m in range(len(pieces))] and None)


def gram(readings, values, counts, prior_root, prior_info, sent):
    cap, width = readings.shape
    whole = pl.BlockSpec(memory_space=pltpu.VMEM)
    left_there = pl.BlockSpec(memory_space=pl.ANY)
    in_hbm = pl.BlockSpec(memory_space=pltpu.HBM)
    n_parts = len(row_cuts(cap))
    return pl.pallas_call(
        functools.partial(gram_kernel, sent),
        in_specs=[pl.BlockSpec(memory_space=pltpu.SMEM), in_hbm, whole, whole, whole],
        out_specs=[left_there] * 2,
        out_shape=[jax.ShapeDtypeStruct((sent // 2, NB), F32)] * 2,
        scratch_shapes=[
            pltpu.VMEM((cap, width), BF16),
            pltpu.VMEM((sent, NB), F32),
            pltpu.VMEM((width, width), F32),
            pltpu.VMEM((8, width), F32),
            pltpu.SemaphoreType.DMA((n_parts,)),
            pltpu.SemaphoreType.DMA((width // NB,)),
        ],
        compiler_params=vmem(60),
        name="gram",
    )(counts, readings, values, prior_root, prior_info.reshape(1, -1))


def lane_of(v, at):
    return jnp.broadcast_to(v[:, at : at + 1], v.shape)


def row_of(v, at):
    return jnp.broadcast_to(v[at : at + 1, :], v.shape)


PANEL, STRIP = 16, 32


def factor_block(read, write, other_work):
    lane = lax.broadcasted_iota(jnp.int32, (8, NB), 1)
    sub = lax.broadcasted_iota(jnp.int32, (8, NB), 0)
    groups = NB // 8
    per = STRIP // 8
    a = [read(u) for u in range(groups)]
    for t in range(NB // STRIP):
        s0 = STRIP * t
        w = a[per * t : per * t + per]
        pivot = [None] * per
        for panel in range(STRIP // PANEL):
            g0 = panel * (PANEL // 8)
            c0 = s0 + PANEL * panel
            col = {}
            for k in range(PANEL):
                for i in range(g0 + k // 8, per):
                    col[i, k] = lane_of(w[i], c0 + k)
            next(other_work, None)
            d = row_of(col[g0, 0], 0)
            inv = 1.0 / d
            for k in range(PANEL):
                gk, ks = g0 + k // 8, k % 8
                pivot[gk] = d if ks == 0 else jnp.where(sub == ks, d, pivot[gk])
                below = {v: row_of(col[g0 + v // 8, k], v % 8) for v in range(k + 1, PANEL)}
                if k + 1 < PANEL:
                    ahead = row_of(col[g0 + (k + 1) // 8, k + 1], (k + 1) % 8)
                    d_next = ahead - (below[k + 1] * below[k + 1]) * inv
                    inv_next = 1.0 / d_next
                one = lane == c0 + k
                row = jnp.where(one, 1.0, row_of(w[gk], ks))
                for i in range(gk, per):
                    m = col[i, k] * inv
                    if i == gk:
                        m = jnp.where(sub > ks, m, 0.0)
                    for v in range(k + 1, PANEL):
                        if i >= g0 + v // 8:
                            col[i, v] = col[i, v] - m * below[v]
                    gone = one & (sub > ks) if i == gk else one
                    w[i] = jnp.where(gone, 0.0, w[i]) - m * row
                if k + 1 < PANEL:
                    d, inv = d_next, inv_next
        inside = (lane >= s0) & (lane < s0 + STRIP)
        scaled = []
        for i in range(per):
            scale = lax.rsqrt(pivot[i])
            v = w[i] * scale
            row = sub + (s0 + 8 * i)
            lower = jnp.where(lane < row, v, jnp.where(lane == row, scale, 0.0))
            write(per * t + i, jnp.where(lane >= row, v, 0.0), lower)
            scaled.append(jnp.where(inside, lower, v))
        if s0 + STRIP < NB:
            hi, lo = split(jnp.concatenate(scaled, axis=0))
            off = dot_t(jnp.concatenate([hi, hi, lo], axis=0), jnp.concatenate([hi, lo, hi], axis=0))
            for i in range(per * (t + 1), groups):
                a[i] = jnp.where(inside, 0.0, a[i]) - off[8 * i : 8 * i + 8, :]


def three(hi, lo, axis):
    return jnp.concatenate([hi, hi, lo], axis=axis)


def three_other(hi, lo, axis):
    return jnp.concatenate([hi, lo, hi], axis=axis)


def factor_kernel(n_quarter, n_layer, own_ref, far_ref, root_ref, info_ref, g, s, minv, r, uhi, ulo, thi, tlo, y):
    width = r.shape[1]
    nb = width // NB
    place = block_at(width)
    blk, layer = lax.axis_index("blk"), lax.axis_index("fibre")
    side, quarter = blk % 2, blk // 2
    piece = own_ref.shape[0] // (n_quarter * n_layer)
    for ms in range(n_quarter):
        for mz in range(n_layer):
            for mc, ref in enumerate((own_ref, far_ref)):
                to = (((side ^ mc) * n_quarter + (quarter ^ ms)) * n_layer + (layer ^ mz)) * piece
                at = (ms * n_layer + mz) * piece
                g[pl.ds(pl.multiple_of(to, 8), piece), :] = ref[at : at + piece, :]

    def block(i, j):
        return g[place[i, j] * NB : place[i, j] * NB + NB, :]

    def span(i):
        return slice(i * NB, i * NB + NB)

    hw = NB // 2
    corner = g[0:NB, :]
    mirror = corner.T
    for b in range(2 * nb):
        y[:, b * hw : (b + 1) * hw] = jnp.broadcast_to(corner[hw + b : hw + b + 1, 0:hw], (8, hw))
    lane = lax.broadcasted_iota(jnp.int32, (hw, NB), 1)
    s[0:hw, 0:NB] = corner[0:hw, :]
    s[hw:NB, 0:NB] = jnp.where(lane < hw, mirror[hw:, :], corner[hw:, :])
    def inverse(i):
        return split(minv[span(i), :])

    def solve(i, c):
        mh, ml = inverse(i)
        sh, sl = split(s[span(i), c])
        u = jnp.dot(three(mh, ml, 1), three_other(sh, sl, 0), preferred_element_type=F32)
        r[span(i), c] = u
        uh, ul = split(u)
        uhi[span(i), c] = uh
        ulo[span(i), c] = ul
        return uh, ul

    def turn(i, b):
        th, tl = split(r[span(i), span(b)].T)
        thi[span(b), span(i)] = th
        tlo[span(b), span(i)] = tl

    def reduce(i, c, rows):
        up = slice(0, rows * NB)
        off = jnp.dot(
            three(thi[span(i), up], tlo[span(i), up], 1),
            three_other(uhi[up, c], ulo[up, c], 0),
            preferred_element_type=F32,
        )
        for b in range(c.start // NB, c.stop // NB):
            s[span(i), span(b)] = block(i, b) - off[:, b * NB - c.start : b * NB - c.start + NB]

    def rest_of(i):
        cuts = [slice(c, min(c + 2 * NB, width)) for c in range((i + 2) * NB, width, 2 * NB)]
        for c in cuts:
            solve(i, c)
            yield
        if i + 2 < nb:
            turn(i, i + 1)
            turn(i, i + 2)
            reduce(i + 2, span(i + 2), i + 1)
            yield
        for c in cuts:
            reduce(i + 1, c, i + 1)
            yield
        for b in range(i + 3, nb):
            turn(i, b)
        mh, ml = inverse(i)
        bh, bl = split(y[:, span(i)])
        yi = lax.dot_general(
            three(bh, bl, 1), three_other(mh, ml, 1), (((1,), (1,)), ((), ())), preferred_element_type=F32
        )
        y[:, span(i)] = yi
        yield
        if i + 1 < nb:
            c = slice((i + 1) * NB, width)
            yh, yl = split(yi)
            y[:, c] -= jnp.dot(
                three(yh, yl, 1), three_other(uhi[span(i), c], ulo[span(i), c], 0), preferred_element_type=F32
            )
            yield
        if i:
            r[span(i), 0 : i * NB] = jnp.zeros((NB, i * NB), F32)
            yield

    other_work = iter(())
    for i in range(nb):

        def read(u):
            return s[i * NB + 8 * u : i * NB + 8 * u + 8, span(i)]

        def write(u, upper, lower):
            at = slice(i * NB + 8 * u, i * NB + 8 * u + 8)
            r[at, span(i)] = upper
            minv[at, :] = lower

        factor_block(read, write, other_work)
        for _ in other_work:
            pass
        if i == 0:
            for b in range(1, nb):
                s[span(0), span(b)] = block(0, b)
        if i + 1 < nb:
            uh, ul = solve(i, span(i + 1))
            at = slice((i + 1) * NB, (i + 2) * NB)
            have = s[at, at] if i else block(1, 1)
            s[at, at] = have - dot_t(three(uh, ul, 0), three_other(uh, ul, 0))
        other_work = rest_of(i)
    for _ in other_work:
        pass
    rows = root_ref.shape[0]
    root_ref[...] = r[pl.ds(pl.multiple_of(blk * rows, 8), rows), :]
    for b in range(nb):
        info_ref[b : b + 1, :] = y[0:1, span(b)]


def factor(own, far, n_quarter, n_layer, width, rows):
    whole = pl.BlockSpec(memory_space=pltpu.VMEM)
    nb = width // NB
    return pl.pallas_call(
        functools.partial(factor_kernel, n_quarter, n_layer),
        in_specs=[whole] * 2,
        out_specs=[whole] * 2,
        out_shape=[jax.ShapeDtypeStruct((rows, width), F32), jax.ShapeDtypeStruct((nb, NB), F32)],
        scratch_shapes=[
            pltpu.VMEM((2 * own.shape[0], NB), F32),
            pltpu.VMEM((width, width), F32),
            pltpu.VMEM((width, NB), F32),
            pltpu.VMEM((width, width), F32),
        ]
        + [pltpu.VMEM((width, width), BF16)] * 4
        + [pltpu.VMEM((8, width), F32)],
        compiler_params=vmem(28),
        name="factor",
    )(own, far)


def swap(x, axis, mask):
    n = lax.axis_size(axis)
    return lax.ppermute(x, axis, [(d, d ^ mask) for d in range(n)])


def shares(parts, count, me):
    rows = parts[0].shape[0] // count
    return [
        functools.reduce(lambda a, b: a + b, [lax.dynamic_slice_in_dim(x, (me ^ m) * rows, rows, 0) for x in parts])
        for m in range(count)
    ]


def trade(mine, axis, masks):
    return [mine[0]] + [swap(x, axis, m) for x, m in zip(mine[1:], masks)]


def gather(x, axis, masks):
    return jnp.concatenate([x] + [swap(x, axis, m) for m in masks], axis=0)


def local(readings, values, counts, prior_root, prior_info):
    width = readings.shape[1]
    n_blk, n_fibre = lax.axis_size("blk"), lax.axis_size("fibre")
    blk, fibre = lax.axis_index("blk"), lax.axis_index("fibre")
    n_quarter = n_blk // 2
    quarters = [2 * m for m in range(1, n_quarter)]
    layers = list(range(1, n_fibre))
    unit = 8 * n_blk * n_fibre
    nb = width // NB
    sent = -(-(nb * (nb + 1) // 2 * NB) // unit) * unit

    keep, send = gram(readings, values, counts, prior_root, prior_info, sent)
    parts = [keep, swap(send, "blk", 1)]
    parts = trade(shares(parts, n_quarter, blk // 2), "blk", quarters)
    parts = trade(shares(parts, n_fibre, fibre), "fibre", layers)
    own = functools.reduce(lambda x, y: x + y, parts)
    own = gather(gather(own, "fibre", layers), "blk", quarters)
    far = swap(own, "blk", 1)
    root, info = factor(own, far, n_quarter, n_fibre, width, width // n_blk)
    return root, info.reshape(width)


def solution(mesh):
    placed = (
        P(("fibre", "blk"), None),
        P(("fibre", "blk")),
        P(("fibre", "blk")),
        P(("fibre", "blk"), None),
        P(("fibre", "blk")),
    )
    return jax.shard_map(
        local, mesh=mesh, in_specs=placed, out_specs=(P("blk", None), P()), check_vma=False
    )
```

```python
import functools

import jax
import jax.numpy as jnp
from jax import lax
from jax.experimental import pallas as pl
from jax.experimental.pallas import tpu as pltpu
from jax.sharding import PartitionSpec as P

F32 = jnp.float32
BF16 = jnp.bfloat16
NB = 128


def vmem(mib):
    return pltpu.CompilerParams(vmem_limit_bytes=mib * 2**20)


def split(x):
    hi = x.astype(BF16)
    return hi, (x - hi.astype(F32)).astype(BF16)


def block_at(width):
    nb = width // NB
    places, at = {}, 0
    for i in range(nb):
        for j in range(i, nb):
            places[i, j] = at
            at += 1
    return places


def dot_t(a, b):
    return lax.dot_general(a, b, (((0,), (0,)), ((), ())), preferred_element_type=F32)


def row_cuts(cap):
    cuts = [0, cap // 8, 3 * cap // 8, 5 * cap // 8, cap]
    return list(zip(cuts[:-1], cuts[1:])) if cap % 128 == 0 else [(0, cap)]


def gram_kernel(sent, count_ref, rows_ref, vals_ref, prior_ref, pinfo_ref, keep_ref, send_ref, x, stage, acc, info, sem):
    cap, width = rows_ref.shape
    nb = width // NB
    half = sent // 2
    total = nb * (nb + 1) // 2 * NB
    tile = min(2 * NB, width)
    tiles = [(i, i + tile) for i in range(0, width, tile)]
    parts = row_cuts(cap)
    copies = [
        pltpu.make_async_copy(rows_ref.at[pl.ds(lo, hi - lo), :], x.at[pl.ds(lo, hi - lo), :], sem.at[n])
        for n, (lo, hi) in enumerate(parts)
    ]
    for copy in copies:
        copy.start()

    p = prior_ref[...]
    hi = p.astype(BF16)
    rest = p - hi.astype(F32)
    mid = rest.astype(BF16)
    lo = (rest - mid.astype(F32)).astype(BF16)
    left = jnp.concatenate([hi, hi, mid, mid, hi, lo], axis=0)
    right = jnp.concatenate([hi, mid, hi, mid, lo, hi], axis=0)
    for i, j in tiles:
        acc[i:j, i:] = dot_t(left[:, i:j], right[:, i:])
    info[...] = jnp.broadcast_to(
        jnp.dot(pinfo_ref[...], p, precision=lax.Precision.HIGHEST, preferred_element_type=F32), info.shape
    )
    for row in range(total, sent, NB):
        stage[row : row + NB, :] = jnp.zeros((NB, NB), F32)

    place = block_at(width)
    side = lax.axis_index("blk") % 2

    def on_each_side(do):
        for at_side in range(2):
            pl.when(side == at_side)(functools.partial(do, at_side))

    for n, (lo, hi) in enumerate(parts):
        copies[n].wait()
        live = count_ref[0] - lo

        @pl.when(live < hi - lo)
        def _():
            row = lax.broadcasted_iota(jnp.int32, (hi - lo, 1), 0)
            x[lo:hi, :] = jnp.where(row < live, x[lo:hi, :], jnp.zeros((), BF16))

        v = vals_ref[lo:hi].astype(F32).reshape(1, hi - lo)
        v = jnp.broadcast_to(v, (16, hi - lo)).astype(BF16)
        for i, j in tiles:
            if i == 0:
                left = jnp.concatenate([x[lo:hi, i:j].T, v], axis=0)
                both = jnp.dot(left, x[lo:hi, :], preferred_element_type=F32)
                term = acc[i:j, i:] + both[0 : j - i, :]
                info[...] += both[j - i : j - i + 8, :]
            else:
                term = acc[i:j, i:] + dot_t(x[lo:hi, i:j], x[lo:hi, i:])
            if n + 1 < len(parts):
                acc[i:j, i:] = term
                continue
            for bi in range(i // NB, j // NB):
                for bj in range(bi, nb):
                    at = place[bi, bj] * NB
                    stage[at : at + NB, :] = term[bi * NB - i : bi * NB - i + NB, bj * NB - i : bj * NB - i + NB]
            if i == 0:
                hw = NB // 2
                for b in range(2 * nb):
                    stage[hw + b : hw + b + 1, 0:hw] = info[0:1, b * hw : (b + 1) * hw]

    def give(at_side):
        halves = (keep_ref, send_ref) if at_side == 0 else (send_ref, keep_ref)
        for n, ref in enumerate(halves):
            ref[...] = stage[n * half : (n + 1) * half, :]

    on_each_side(give)


def gram(readings, values, counts, prior_root, prior_info, sent):
    cap, width = readings.shape
    whole = pl.BlockSpec(memory_space=pltpu.VMEM)
    left_there = pl.BlockSpec(memory_space=pl.ANY)
    in_hbm = pl.BlockSpec(memory_space=pltpu.HBM)
    n_parts = len(row_cuts(cap))
    return pl.pallas_call(
        functools.partial(gram_kernel, sent),
        in_specs=[pl.BlockSpec(memory_space=pltpu.SMEM), in_hbm, whole, whole, whole],
        out_specs=[whole] * 2,
        out_shape=[jax.ShapeDtypeStruct((sent // 2, NB), F32)] * 2,
        scratch_shapes=[
            pltpu.VMEM((cap, width), BF16),
            pltpu.VMEM((sent, NB), F32),
            pltpu.VMEM((width, width), F32),
            pltpu.VMEM((8, width), F32),
            pltpu.SemaphoreType.DMA((n_parts,)),
        ],
        compiler_params=vmem(24),
        name="gram",
    )(counts, *(pltpu.with_memory_space_constraint(x, pltpu.HBM) for x in (readings, values, prior_root, prior_info.reshape(1, -1))))


def lane_of(v, at):
    return jnp.broadcast_to(v[:, at : at + 1], v.shape)


def row_of(v, at):
    return jnp.broadcast_to(v[at : at + 1, :], v.shape)


PANEL, STRIP = 16, 32


def factor_block(read, write, other_work):
    lane = lax.broadcasted_iota(jnp.int32, (8, NB), 1)
    sub = lax.broadcasted_iota(jnp.int32, (8, NB), 0)
    groups = NB // 8
    per = STRIP // 8
    a = [read(u) for u in range(groups)]
    for t in range(NB // STRIP):
        s0 = STRIP * t
        w = a[per * t : per * t + per]
        pivot = [None] * per
        for panel in range(STRIP // PANEL):
            g0 = panel * (PANEL // 8)
            c0 = s0 + PANEL * panel
            col = {}
            for k in range(PANEL):
                for i in range(g0 + k // 8, per):
                    col[i, k] = lane_of(w[i], c0 + k)
            next(other_work, None)
            d = row_of(col[g0, 0], 0)
            inv = 1.0 / d
            for k in range(PANEL):
                gk, ks = g0 + k // 8, k % 8
                pivot[gk] = d if ks == 0 else jnp.where(sub == ks, d, pivot[gk])
                below = {v: row_of(col[g0 + v // 8, k], v % 8) for v in range(k + 1, PANEL)}
                if k + 1 < PANEL:
                    ahead = row_of(col[g0 + (k + 1) // 8, k + 1], (k + 1) % 8)
                    d_next = ahead - (below[k + 1] * below[k + 1]) * inv
                    inv_next = 1.0 / d_next
                one = lane == c0 + k
                row = jnp.where(one, 1.0, row_of(w[gk], ks))
                for i in range(gk, per):
                    m = col[i, k] * inv
                    if i == gk:
                        m = jnp.where(sub > ks, m, 0.0)
                    for v in range(k + 1, PANEL):
                        if i >= g0 + v // 8:
                            col[i, v] = col[i, v] - m * below[v]
                    gone = one & (sub > ks) if i == gk else one
                    w[i] = jnp.where(gone, 0.0, w[i]) - m * row
                if k + 1 < PANEL:
                    d, inv = d_next, inv_next
        inside = (lane >= s0) & (lane < s0 + STRIP)
        scaled = []
        for i in range(per):
            scale = lax.rsqrt(pivot[i])
            v = w[i] * scale
            row = sub + (s0 + 8 * i)
            lower = jnp.where(lane < row, v, jnp.where(lane == row, scale, 0.0))
            write(per * t + i, jnp.where(lane >= row, v, 0.0), lower)
            scaled.append(jnp.where(inside, lower, v))
        if s0 + STRIP < NB:
            hi, lo = split(jnp.concatenate(scaled, axis=0))
            off = dot_t(jnp.concatenate([hi, hi, lo], axis=0), jnp.concatenate([hi, lo, hi], axis=0))
            for i in range(per * (t + 1), groups):
                a[i] = jnp.where(inside, 0.0, a[i]) - off[8 * i : 8 * i + 8, :]


def three(hi, lo, axis):
    return jnp.concatenate([hi, hi, lo], axis=axis)


def three_other(hi, lo, axis):
    return jnp.concatenate([hi, lo, hi], axis=axis)


def factor_kernel(n_quarter, n_layer, own_ref, far_ref, root_ref, info_ref, g, s, minv, r, uhi, ulo, thi, tlo, y):
    width = r.shape[1]
    nb = width // NB
    place = block_at(width)
    blk, layer = lax.axis_index("blk"), lax.axis_index("fibre")
    side, quarter = blk % 2, blk // 2
    piece = own_ref.shape[0] // (n_quarter * n_layer)
    for ms in range(n_quarter):
        for mz in range(n_layer):
            for mc, ref in enumerate((own_ref, far_ref)):
                to = (((side ^ mc) * n_quarter + (quarter ^ ms)) * n_layer + (layer ^ mz)) * piece
                at = (ms * n_layer + mz) * piece
                g[pl.ds(pl.multiple_of(to, 8), piece), :] = ref[at : at + piece, :]

    def block(i, j):
        return g[place[i, j] * NB : place[i, j] * NB + NB, :]

    def span(i):
        return slice(i * NB, i * NB + NB)

    hw = NB // 2
    corner = g[0:NB, :]
    mirror = corner.T
    for b in range(2 * nb):
        y[:, b * hw : (b + 1) * hw] = jnp.broadcast_to(corner[hw + b : hw + b + 1, 0:hw], (8, hw))
    lane = lax.broadcasted_iota(jnp.int32, (hw, NB), 1)
    s[0:hw, 0:NB] = corner[0:hw, :]
    s[hw:NB, 0:NB] = jnp.where(lane < hw, mirror[hw:, :], corner[hw:, :])
    def inverse(i):
        return split(minv[span(i), :])

    def solve(i, c):
        mh, ml = inverse(i)
        sh, sl = split(s[span(i), c])
        u = jnp.dot(three(mh, ml, 1), three_other(sh, sl, 0), preferred_element_type=F32)
        r[span(i), c] = u
        uh, ul = split(u)
        uhi[span(i), c] = uh
        ulo[span(i), c] = ul
        return uh, ul

    def turn(i, b):
        th, tl = split(r[span(i), span(b)].T)
        thi[span(b), span(i)] = th
        tlo[span(b), span(i)] = tl

    def reduce(i, c, rows):
        up = slice(0, rows * NB)
        off = jnp.dot(
            three(thi[span(i), up], tlo[span(i), up], 1),
            three_other(uhi[up, c], ulo[up, c], 0),
            preferred_element_type=F32,
        )
        for b in range(c.start // NB, c.stop // NB):
            s[span(i), span(b)] = block(i, b) - off[:, b * NB - c.start : b * NB - c.start + NB]

    def rest_of(i):
        cuts = [slice(c, min(c + 2 * NB, width)) for c in range((i + 2) * NB, width, 2 * NB)]
        for c in cuts:
            solve(i, c)
            yield
        if i + 2 < nb:
            turn(i, i + 1)
            turn(i, i + 2)
            reduce(i + 2, span(i + 2), i + 1)
            yield
        for c in cuts:
            reduce(i + 1, c, i + 1)
            yield
        for b in range(i + 3, nb):
            turn(i, b)
        mh, ml = inverse(i)
        bh, bl = split(y[:, span(i)])
        yi = lax.dot_general(
            three(bh, bl, 1), three_other(mh, ml, 1), (((1,), (1,)), ((), ())), preferred_element_type=F32
        )
        y[:, span(i)] = yi
        yield
        if i + 1 < nb:
            c = slice((i + 1) * NB, width)
            yh, yl = split(yi)
            y[:, c] -= jnp.dot(
                three(yh, yl, 1), three_other(uhi[span(i), c], ulo[span(i), c], 0), preferred_element_type=F32
            )
            yield
        if i:
            r[span(i), 0 : i * NB] = jnp.zeros((NB, i * NB), F32)
            yield

    other_work = iter(())
    for i in range(nb):

        def read(u):
            return s[i * NB + 8 * u : i * NB + 8 * u + 8, span(i)]

        def write(u, upper, lower):
            at = slice(i * NB + 8 * u, i * NB + 8 * u + 8)
            r[at, span(i)] = upper
            minv[at, :] = lower

        factor_block(read, write, other_work)
        for _ in other_work:
            pass
        if i == 0:
            for b in range(1, nb):
                s[span(0), span(b)] = block(0, b)
        if i + 1 < nb:
            uh, ul = solve(i, span(i + 1))
            at = slice((i + 1) * NB, (i + 2) * NB)
            have = s[at, at] if i else block(1, 1)
            s[at, at] = have - dot_t(three(uh, ul, 0), three_other(uh, ul, 0))
        other_work = rest_of(i)
    for _ in other_work:
        pass
    rows = root_ref.shape[0]
    root_ref[...] = r[pl.ds(pl.multiple_of(blk * rows, 8), rows), :]
    for b in range(nb):
        info_ref[b : b + 1, :] = y[0:1, span(b)]


def factor(own, far, n_quarter, n_layer, width, rows):
    whole = pl.BlockSpec(memory_space=pltpu.VMEM)
    nb = width // NB
    return pl.pallas_call(
        functools.partial(factor_kernel, n_quarter, n_layer),
        in_specs=[whole] * 2,
        out_specs=[whole] * 2,
        out_shape=[jax.ShapeDtypeStruct((rows, width), F32), jax.ShapeDtypeStruct((nb, NB), F32)],
        scratch_shapes=[
            pltpu.VMEM((2 * own.shape[0], NB), F32),
            pltpu.VMEM((width, width), F32),
            pltpu.VMEM((width, NB), F32),
            pltpu.VMEM((width, width), F32),
        ]
        + [pltpu.VMEM((width, width), BF16)] * 4
        + [pltpu.VMEM((8, width), F32)],
        compiler_params=vmem(28),
        name="factor",
    )(own, far)


def swap(x, axis, mask):
    n = lax.axis_size(axis)
    return lax.ppermute(x, axis, [(d, d ^ mask) for d in range(n)])


def shares(parts, count, me):
    rows = parts[0].shape[0] // count
    return [
        functools.reduce(lambda a, b: a + b, [lax.dynamic_slice_in_dim(x, (me ^ m) * rows, rows, 0) for x in parts])
        for m in range(count)
    ]


def trade(mine, axis, masks):
    return [mine[0]] + [swap(x, axis, m) for x, m in zip(mine[1:], masks)]


def gather(x, axis, masks):
    return jnp.concatenate([x] + [swap(x, axis, m) for m in masks], axis=0)


def local(readings, values, counts, prior_root, prior_info):
    width = readings.shape[1]
    n_blk, n_fibre = lax.axis_size("blk"), lax.axis_size("fibre")
    blk, fibre = lax.axis_index("blk"), lax.axis_index("fibre")
    n_quarter = n_blk // 2
    quarters = [2 * m for m in range(1, n_quarter)]
    layers = list(range(1, n_fibre))
    unit = 8 * n_blk * n_fibre
    nb = width // NB
    sent = -(-(nb * (nb + 1) // 2 * NB) // unit) * unit

    keep, send = gram(readings, values, counts, prior_root, prior_info, sent)
    parts = [keep, swap(send, "blk", 1)]
    parts = trade(shares(parts, n_quarter, blk // 2), "blk", quarters)
    parts = trade(shares(parts, n_fibre, fibre), "fibre", layers)
    own = functools.reduce(lambda x, y: x + y, parts)
    own = gather(gather(own, "fibre", layers), "blk", quarters)
    far = swap(own, "blk", 1)
    root, info = factor(own, far, n_quarter, n_fibre, width, width // n_blk)
    return root, info.reshape(width)


def solution(mesh):
    placed = (
        P(("fibre", "blk"), None),
        P(("fibre", "blk")),
        P(("fibre", "blk")),
        P(("fibre", "blk"), None),
        P(("fibre", "blk")),
    )
    return jax.shard_map(
        local, mesh=mesh, in_specs=placed, out_specs=(P("blk", None), P()), check_vma=False
    )
```

```python
import functools

import jax
import jax.numpy as jnp
from jax import lax
from jax.experimental import pallas as pl
from jax.experimental.pallas import tpu as pltpu
from jax.sharding import PartitionSpec as P

F32 = jnp.float32
BF16 = jnp.bfloat16
NB = 128


def vmem(mib):
    return pltpu.CompilerParams(vmem_limit_bytes=mib * 2**20)


def split(x):
    hi = x.astype(BF16)
    return hi, (x - hi.astype(F32)).astype(BF16)


def packed_rows(width):
    nb = width // NB
    rows, at = {}, 0
    for t in range(0, nb, 2):
        for i in (t, t + 1):
            for j in range(i + 1, nb):
                rows[i, j] = at
                at += NB
        for part in ((t, "top"), (t + 1, "top"), (t, "corner")):
            rows[part] = at
            at += NB // 2
    return rows, at


def dot_t(a, b):
    return lax.dot_general(a, b, (((0,), (0,)), ((), ())), preferred_element_type=F32)


def row_cuts(cap):
    cuts = [0, cap // 8, 3 * cap // 8, 5 * cap // 8, cap]
    return list(zip(cuts[:-1], cuts[1:])) if cap % 128 == 0 else [(0, cap)]


def gram_kernel(sent, count_ref, rows_ref, vals_ref, prior_ref, pinfo_ref, keep_ref, send_ref, x, stage, acc, info, sem):
    cap, width = rows_ref.shape
    nb = width // NB
    half = sent // 2
    place, total = packed_rows(width)
    tile = 2 * NB
    tiles = [(i, i + tile) for i in range(0, width, tile)]
    parts = row_cuts(cap)
    copies = [
        pltpu.make_async_copy(rows_ref.at[pl.ds(lo, hi - lo), :], x.at[pl.ds(lo, hi - lo), :], sem.at[n])
        for n, (lo, hi) in enumerate(parts)
    ]
    for copy in copies:
        copy.start()

    p = prior_ref[...]
    hi = p.astype(BF16)
    rest = p - hi.astype(F32)
    mid = rest.astype(BF16)
    lo = (rest - mid.astype(F32)).astype(BF16)
    left = jnp.concatenate([hi, hi, mid, mid, hi, lo], axis=0)
    right = jnp.concatenate([hi, mid, hi, mid, lo, hi], axis=0)
    for i, j in tiles:
        acc[i:j, i:] = dot_t(left[:, i:j], right[:, i:])
    info[...] = jnp.broadcast_to(
        jnp.dot(pinfo_ref[...], p, precision=lax.Precision.HIGHEST, preferred_element_type=F32), info.shape
    )
    if sent > total:
        stage[total:sent, :] = jnp.zeros((sent - total, NB), F32)

    side = lax.axis_index("blk") % 2

    def on_each_side(do):
        for at_side in range(2):
            pl.when(side == at_side)(functools.partial(do, at_side))

    for n, (lo, hi) in enumerate(parts):
        copies[n].wait()
        live = count_ref[0] - lo

        @pl.when(live < hi - lo)
        def _():
            row = lax.broadcasted_iota(jnp.int32, (hi - lo, 1), 0)
            x[lo:hi, :] = jnp.where(row < live, x[lo:hi, :], jnp.zeros((), BF16))

        v = vals_ref[lo:hi].astype(F32).reshape(1, hi - lo)
        v = jnp.broadcast_to(v, (16, hi - lo)).astype(BF16)
        for i, j in tiles:
            if i == 0:
                left = jnp.concatenate([x[lo:hi, i:j].T, v], axis=0)
                both = jnp.dot(left, x[lo:hi, :], preferred_element_type=F32)
                term = acc[i:j, i:] + both[0 : j - i, :]
                info[...] += both[j - i : j - i + 8, :]
            else:
                term = acc[i:j, i:] + dot_t(x[lo:hi, i:j], x[lo:hi, i:])
            if n + 1 < len(parts):
                acc[i:j, i:] = term
                continue
            hw = NB // 2
            first = i // NB
            for bi in (first, first + 1):
                up = bi * NB - i
                for bj in range(bi + 1, nb):
                    at = place[bi, bj]
                    stage[at : at + NB, :] = term[up : up + NB, bj * NB - i : bj * NB - i + NB]
                at = place[bi, "top"]
                stage[at : at + hw, :] = term[up : up + hw, up : up + NB]
            at = place[first, "corner"]
            stage[at : at + hw, :] = jnp.concatenate(
                [term[hw:NB, hw:NB], term[NB + hw : 2 * NB, NB + hw : 2 * NB]], axis=1
            )
            if i == 0:
                q = NB // 4
                at = place[0, "top"] + q
                for b in range(width // q):
                    stage[at + b : at + b + 1, 0:q] = info[0:1, b * q : (b + 1) * q]

    def give(at_side):
        halves = (keep_ref, send_ref) if at_side == 0 else (send_ref, keep_ref)
        for n, ref in enumerate(halves):
            ref[...] = stage[n * half : (n + 1) * half, :]

    on_each_side(give)


def gram(readings, values, counts, prior_root, prior_info, sent):
    cap, width = readings.shape
    whole = pl.BlockSpec(memory_space=pltpu.VMEM)
    left_there = pl.BlockSpec(memory_space=pl.ANY)
    in_hbm = pl.BlockSpec(memory_space=pltpu.HBM)
    n_parts = len(row_cuts(cap))
    return pl.pallas_call(
        functools.partial(gram_kernel, sent),
        in_specs=[pl.BlockSpec(memory_space=pltpu.SMEM), in_hbm, whole, whole, whole],
        out_specs=[whole] * 2,
        out_shape=[jax.ShapeDtypeStruct((sent // 2, NB), F32)] * 2,
        scratch_shapes=[
            pltpu.VMEM((cap, width), BF16),
            pltpu.VMEM((sent, NB), F32),
            pltpu.VMEM((width, width), F32),
            pltpu.VMEM((8, width), F32),
            pltpu.SemaphoreType.DMA((n_parts,)),
        ],
        compiler_params=vmem(24),
        name="gram",
    )(counts, *(pltpu.with_memory_space_constraint(x, pltpu.HBM) for x in (readings, values, prior_root, prior_info.reshape(1, -1))))


def lane_of(v, at):
    return jnp.broadcast_to(v[:, at : at + 1], v.shape)


def row_of(v, at):
    return jnp.broadcast_to(v[at : at + 1, :], v.shape)


PANEL, STRIP = 16, 32


def factor_block(read, write, other_work):
    lane = lax.broadcasted_iota(jnp.int32, (8, NB), 1)
    sub = lax.broadcasted_iota(jnp.int32, (8, NB), 0)
    groups = NB // 8
    per = STRIP // 8
    a = [read(u) for u in range(groups)]
    for t in range(NB // STRIP):
        s0 = STRIP * t
        w = a[per * t : per * t + per]
        pivot = [None] * per
        for panel in range(STRIP // PANEL):
            g0 = panel * (PANEL // 8)
            c0 = s0 + PANEL * panel
            col = {}
            for k in range(PANEL):
                for i in range(g0 + k // 8, per):
                    col[i, k] = lane_of(w[i], c0 + k)
            next(other_work, None)
            d = row_of(col[g0, 0], 0)
            inv = 1.0 / d
            for k in range(PANEL):
                gk, ks = g0 + k // 8, k % 8
                pivot[gk] = d if ks == 0 else jnp.where(sub == ks, d, pivot[gk])
                below = {v: row_of(col[g0 + v // 8, k], v % 8) for v in range(k + 1, PANEL)}
                if k + 1 < PANEL:
                    ahead = row_of(col[g0 + (k + 1) // 8, k + 1], (k + 1) % 8)
                    d_next = ahead - (below[k + 1] * below[k + 1]) * inv
                    inv_next = 1.0 / d_next
                one = lane == c0 + k
                row = jnp.where(one, 1.0, row_of(w[gk], ks))
                for i in range(gk, per):
                    m = col[i, k] * inv
                    if i == gk:
                        m = jnp.where(sub > ks, m, 0.0)
                    for v in range(k + 1, PANEL):
                        if i >= g0 + v // 8:
                            col[i, v] = col[i, v] - m * below[v]
                    gone = one & (sub > ks) if i == gk else one
                    w[i] = jnp.where(gone, 0.0, w[i]) - m * row
                if k + 1 < PANEL:
                    d, inv = d_next, inv_next
        inside = (lane >= s0) & (lane < s0 + STRIP)
        scaled = []
        for i in range(per):
            scale = lax.rsqrt(pivot[i])
            v = w[i] * scale
            row = sub + (s0 + 8 * i)
            lower = jnp.where(lane < row, v, jnp.where(lane == row, scale, 0.0))
            write(per * t + i, jnp.where(lane >= row, v, 0.0), lower)
            scaled.append(jnp.where(inside, lower, v))
        if s0 + STRIP < NB:
            hi, lo = split(jnp.concatenate(scaled, axis=0))
            off = dot_t(jnp.concatenate([hi, hi, lo], axis=0), jnp.concatenate([hi, lo, hi], axis=0))
            for i in range(per * (t + 1), groups):
                a[i] = jnp.where(inside, 0.0, a[i]) - off[8 * i : 8 * i + 8, :]


def three(hi, lo, axis):
    return jnp.concatenate([hi, hi, lo], axis=axis)


def three_other(hi, lo, axis):
    return jnp.concatenate([hi, lo, hi], axis=axis)


def factor_kernel(n_quarter, n_layer, own_ref, far_ref, root_ref, info_ref, g, s, minv, r, uhi, ulo, thi, tlo, y):
    width = r.shape[1]
    nb = width // NB
    place, _ = packed_rows(width)
    blk, layer = lax.axis_index("blk"), lax.axis_index("fibre")
    side, quarter = blk % 2, blk // 2
    piece = own_ref.shape[0] // (n_quarter * n_layer)
    for ms in range(n_quarter):
        for mz in range(n_layer):
            for mc, ref in enumerate((own_ref, far_ref)):
                to = (((side ^ mc) * n_quarter + (quarter ^ ms)) * n_layer + (layer ^ mz)) * piece
                at = (ms * n_layer + mz) * piece
                g[pl.ds(pl.multiple_of(to, 8), piece), :] = ref[at : at + piece, :]

    hw, q = NB // 2, NB // 4

    def block(i, j):
        if i != j:
            return g[place[i, j] : place[i, j] + NB, :]
        at = place[i, "top"]
        top = g[at : at + hw, :]
        at = place[i - i % 2, "corner"]
        corner = g[at : at + hw, :]
        mirror = jnp.concatenate([top, top], axis=0).T
        lane = lax.broadcasted_iota(jnp.int32, (hw, NB), 1)
        if i % 2 == 0:
            corner = jnp.concatenate([corner[:, hw:], corner[:, :hw]], axis=1)
        if i == 0:
            row = lax.broadcasted_iota(jnp.int32, (hw, NB), 0)
            top = jnp.where((lane < q) & (row >= q), mirror[:hw, :], top)
        return jnp.concatenate([top, jnp.where(lane < hw, mirror[hw:, :], corner)], axis=0)

    def span(i):
        return slice(i * NB, i * NB + NB)

    for b in range(width // q):
        at = place[0, "top"] + q + b
        y[:, b * q : (b + 1) * q] = jnp.broadcast_to(g[at : at + 1, 0:q], (8, q))
    s[span(0), span(0)] = block(0, 0)

    def inverse(i):
        return split(minv[span(i), :])

    def solve(i, c):
        mh, ml = inverse(i)
        sh, sl = split(s[span(i), c])
        u = jnp.dot(three(mh, ml, 1), three_other(sh, sl, 0), preferred_element_type=F32)
        r[span(i), c] = u
        uh, ul = split(u)
        uhi[span(i), c] = uh
        ulo[span(i), c] = ul
        return uh, ul

    def turn(i, b):
        th, tl = split(r[span(i), span(b)].T)
        thi[span(b), span(i)] = th
        tlo[span(b), span(i)] = tl

    def reduce(i, c, rows):
        up = slice(0, rows * NB)
        off = jnp.dot(
            three(thi[span(i), up], tlo[span(i), up], 1),
            three_other(uhi[up, c], ulo[up, c], 0),
            preferred_element_type=F32,
        )
        for b in range(c.start // NB, c.stop // NB):
            s[span(i), span(b)] = block(i, b) - off[:, b * NB - c.start : b * NB - c.start + NB]

    def rest_of(i):
        cuts = [slice(c, min(c + 2 * NB, width)) for c in range((i + 2) * NB, width, 2 * NB)]
        for c in cuts:
            solve(i, c)
            yield
        if i + 2 < nb:
            turn(i, i + 1)
            turn(i, i + 2)
            reduce(i + 2, span(i + 2), i + 1)
            yield
        for c in cuts:
            reduce(i + 1, c, i + 1)
            yield
        for b in range(i + 3, nb):
            turn(i, b)
        mh, ml = inverse(i)
        bh, bl = split(y[:, span(i)])
        yi = lax.dot_general(
            three(bh, bl, 1), three_other(mh, ml, 1), (((1,), (1,)), ((), ())), preferred_element_type=F32
        )
        y[:, span(i)] = yi
        yield
        if i + 1 < nb:
            c = slice((i + 1) * NB, width)
            yh, yl = split(yi)
            y[:, c] -= jnp.dot(
                three(yh, yl, 1), three_other(uhi[span(i), c], ulo[span(i), c], 0), preferred_element_type=F32
            )
            yield
        if i:
            r[span(i), 0 : i * NB] = jnp.zeros((NB, i * NB), F32)
            yield

    def begin():
        s[span(1), span(1)] = block(1, 1)
        yield
        for b in range(1, nb):
            s[span(0), span(b)] = block(0, b)
        yield

    other_work = begin()
    for i in range(nb):

        def read(u):
            return s[i * NB + 8 * u : i * NB + 8 * u + 8, span(i)]

        def write(u, upper, lower):
            at = slice(i * NB + 8 * u, i * NB + 8 * u + 8)
            r[at, span(i)] = upper
            minv[at, :] = lower

        factor_block(read, write, other_work)
        for _ in other_work:
            pass
        if i + 1 < nb:
            uh, ul = solve(i, span(i + 1))
            at = slice((i + 1) * NB, (i + 2) * NB)
            s[at, at] -= dot_t(three(uh, ul, 0), three_other(uh, ul, 0))
        other_work = rest_of(i)
    for _ in other_work:
        pass
    rows = root_ref.shape[0]
    root_ref[...] = r[pl.ds(pl.multiple_of(blk * rows, 8), rows), :]
    for b in range(nb):
        info_ref[b : b + 1, :] = y[0:1, span(b)]


def factor(own, far, n_quarter, n_layer, width, rows):
    whole = pl.BlockSpec(memory_space=pltpu.VMEM)
    nb = width // NB
    return pl.pallas_call(
        functools.partial(factor_kernel, n_quarter, n_layer),
        in_specs=[whole] * 2,
        out_specs=[whole] * 2,
        out_shape=[jax.ShapeDtypeStruct((rows, width), F32), jax.ShapeDtypeStruct((nb, NB), F32)],
        scratch_shapes=[
            pltpu.VMEM((2 * own.shape[0], NB), F32),
            pltpu.VMEM((width, width), F32),
            pltpu.VMEM((width, NB), F32),
            pltpu.VMEM((width, width), F32),
        ]
        + [pltpu.VMEM((width, width), BF16)] * 4
        + [pltpu.VMEM((8, width), F32)],
        compiler_params=vmem(28),
        name="factor",
    )(own, far)


def swap(x, axis, mask):
    n = lax.axis_size(axis)
    return lax.ppermute(x, axis, [(d, d ^ mask) for d in range(n)])


def shares(parts, count, me):
    rows = parts[0].shape[0] // count
    return [
        functools.reduce(lambda a, b: a + b, [lax.dynamic_slice_in_dim(x, (me ^ m) * rows, rows, 0) for x in parts])
        for m in range(count)
    ]


def trade(mine, axis, masks):
    return [mine[0]] + [swap(x, axis, m) for x, m in zip(mine[1:], masks)]


def gather(x, axis, masks):
    return jnp.concatenate([x] + [swap(x, axis, m) for m in masks], axis=0)


def local(readings, values, counts, prior_root, prior_info):
    width = readings.shape[1]
    n_blk, n_fibre = lax.axis_size("blk"), lax.axis_size("fibre")
    blk, fibre = lax.axis_index("blk"), lax.axis_index("fibre")
    n_quarter = n_blk // 2
    quarters = [2 * m for m in range(1, n_quarter)]
    layers = list(range(1, n_fibre))
    unit = 8 * n_blk * n_fibre
    sent = -(-packed_rows(width)[1] // unit) * unit

    keep, send = gram(readings, values, counts, prior_root, prior_info, sent)
    parts = [keep, swap(send, "blk", 1)]
    parts = trade(shares(parts, n_quarter, blk // 2), "blk", quarters)
    parts = trade(shares(parts, n_fibre, fibre), "fibre", layers)
    own = functools.reduce(lambda x, y: x + y, parts)
    own = gather(gather(own, "fibre", layers), "blk", quarters)
    far = swap(own, "blk", 1)
    root, info = factor(own, far, n_quarter, n_fibre, width, width // n_blk)
    return root, info.reshape(width)


def solution(mesh):
    placed = (
        P(("fibre", "blk"), None),
        P(("fibre", "blk")),
        P(("fibre", "blk")),
        P(("fibre", "blk"), None),
        P(("fibre", "blk")),
    )
    return jax.shard_map(
        local, mesh=mesh, in_specs=placed, out_specs=(P("blk", None), P()), check_vma=False
    )
```

```python
import functools

import jax
import jax.numpy as jnp
from jax import lax
from jax.experimental import pallas as pl
from jax.experimental.pallas import tpu as pltpu
from jax.sharding import PartitionSpec as P

F32 = jnp.float32
BF16 = jnp.bfloat16
NB = 128


def vmem(mib):
    return pltpu.CompilerParams(vmem_limit_bytes=mib * 2**20)


def split(x):
    hi = x.astype(BF16)
    return hi, (x - hi.astype(F32)).astype(BF16)


def packed_rows(width):
    nb = width // NB
    rows, at = {}, 0
    for t in range(0, nb, 2):
        for i in (t, t + 1):
            for j in range(i + 1, nb):
                rows[i, j] = at
                at += NB
        for part in ((t, "top"), (t + 1, "top"), (t, "corner")):
            rows[part] = at
            at += NB // 2
    return rows, at


def dot_t(a, b):
    return lax.dot_general(a, b, (((0,), (0,)), ((), ())), preferred_element_type=F32)


def row_cuts(cap):
    cuts = [0, cap // 8, 3 * cap // 8, 5 * cap // 8, cap]
    return list(zip(cuts[:-1], cuts[1:])) if cap % 128 == 0 else [(0, cap)]


def gram_kernel(sent, count_ref, rows_ref, vals_ref, prior_ref, pinfo_ref, keep_ref, send_ref, x, stage, acc, info, sem):
    cap, width = rows_ref.shape
    nb = width // NB
    half = sent // 2
    place, total = packed_rows(width)
    tile = 2 * NB
    tiles = [(i, i + tile) for i in range(0, width, tile)]
    parts = row_cuts(cap)
    copies = [
        pltpu.make_async_copy(rows_ref.at[pl.ds(lo, hi - lo), :], x.at[pl.ds(lo, hi - lo), :], sem.at[n])
        for n, (lo, hi) in enumerate(parts)
    ]
    for copy in copies:
        copy.start()

    p = prior_ref[...]
    hi = p.astype(BF16)
    rest = p - hi.astype(F32)
    mid = rest.astype(BF16)
    lo = (rest - mid.astype(F32)).astype(BF16)
    left = jnp.concatenate([hi, hi, mid, mid, hi, lo], axis=0)
    right = jnp.concatenate([hi, mid, hi, mid, lo, hi], axis=0)
    for i, j in tiles:
        acc[i:j, i:] = dot_t(left[:, i:j], right[:, i:])
    info[...] = jnp.broadcast_to(
        jnp.dot(pinfo_ref[...], p, precision=lax.Precision.HIGHEST, preferred_element_type=F32), info.shape
    )
    if sent > total:
        stage[total:sent, :] = jnp.zeros((sent - total, NB), F32)

    side = lax.axis_index("blk") % 2

    def on_each_side(do):
        for at_side in range(2):
            pl.when(side == at_side)(functools.partial(do, at_side))

    for n, (lo, hi) in enumerate(parts):
        copies[n].wait()
        live = count_ref[0] - lo

        @pl.when(live < hi - lo)
        def _():
            row = lax.broadcasted_iota(jnp.int32, (hi - lo, 1), 0)
            x[lo:hi, :] = jnp.where(row < live, x[lo:hi, :], jnp.zeros((), BF16))

        v = vals_ref[lo:hi].astype(F32).reshape(1, hi - lo)
        v = jnp.broadcast_to(v, (16, hi - lo)).astype(BF16)
        for i, j in tiles:
            if i == 0:
                left = jnp.concatenate([x[lo:hi, i:j].T, v], axis=0)
                both = jnp.dot(left, x[lo:hi, :], preferred_element_type=F32)
                term = acc[i:j, i:] + both[0 : j - i, :]
                info[...] += both[j - i : j - i + 8, :]
            else:
                term = acc[i:j, i:] + dot_t(x[lo:hi, i:j], x[lo:hi, i:])
            if n + 1 < len(parts):
                acc[i:j, i:] = term
                continue
            hw = NB // 2
            first = i // NB
            for bi in (first, first + 1):
                up = bi * NB - i
                for bj in range(bi + 1, nb):
                    at = place[bi, bj]
                    stage[at : at + NB, :] = term[up : up + NB, bj * NB - i : bj * NB - i + NB]
                at = place[bi, "top"]
                stage[at : at + hw, :] = term[up : up + hw, up : up + NB]
            at = place[first, "corner"]
            stage[at : at + hw, :] = jnp.concatenate(
                [term[hw:NB, hw:NB], term[NB + hw : 2 * NB, NB + hw : 2 * NB]], axis=1
            )
            if i == 0:
                q = NB // 4
                at = place[0, "top"] + q
                for b in range(width // q):
                    stage[at + b : at + b + 1, 0:q] = info[0:1, b * q : (b + 1) * q]

    def give(at_side):
        halves = (keep_ref, send_ref) if at_side == 0 else (send_ref, keep_ref)
        for n, ref in enumerate(halves):
            ref[...] = stage[n * half : (n + 1) * half, :]

    on_each_side(give)


def gram(readings, values, counts, prior_root, prior_info, sent):
    cap, width = readings.shape
    whole = pl.BlockSpec(memory_space=pltpu.VMEM)
    left_there = pl.BlockSpec(memory_space=pl.ANY)
    in_hbm = pl.BlockSpec(memory_space=pltpu.HBM)
    n_parts = len(row_cuts(cap))
    return pl.pallas_call(
        functools.partial(gram_kernel, sent),
        in_specs=[pl.BlockSpec(memory_space=pltpu.SMEM), in_hbm, whole, whole, whole],
        out_specs=[whole] * 2,
        out_shape=[jax.ShapeDtypeStruct((sent // 2, NB), F32)] * 2,
        scratch_shapes=[
            pltpu.VMEM((cap, width), BF16),
            pltpu.VMEM((sent, NB), F32),
            pltpu.VMEM((width, width), F32),
            pltpu.VMEM((8, width), F32),
            pltpu.SemaphoreType.DMA((n_parts,)),
        ],
        compiler_params=vmem(24),
        name="gram",
    )(counts, *(pltpu.with_memory_space_constraint(x, pltpu.HBM) for x in (readings, values, prior_root, prior_info.reshape(1, -1))))


def lane_of(v, at):
    return jnp.broadcast_to(v[:, at : at + 1], v.shape)


def row_of(v, at):
    return jnp.broadcast_to(v[at : at + 1, :], v.shape)


PANEL, STRIP = 16, 32


def factor_block(read, write, other_work):
    lane = lax.broadcasted_iota(jnp.int32, (8, NB), 1)
    sub = lax.broadcasted_iota(jnp.int32, (8, NB), 0)
    groups = NB // 8
    per = STRIP // 8
    a = [read(u) for u in range(groups)]
    for t in range(NB // STRIP):
        s0 = STRIP * t
        w = a[per * t : per * t + per]
        pivot = [None] * per
        for panel in range(STRIP // PANEL):
            g0 = panel * (PANEL // 8)
            c0 = s0 + PANEL * panel
            col = {}
            for k in range(PANEL):
                for i in range(g0 + k // 8, per):
                    col[i, k] = lane_of(w[i], c0 + k)
            next(other_work, None)
            d = row_of(col[g0, 0], 0)
            inv = 1.0 / d
            for k in range(PANEL):
                gk, ks = g0 + k // 8, k % 8
                pivot[gk] = d if ks == 0 else jnp.where(sub == ks, d, pivot[gk])
                below = {v: row_of(col[g0 + v // 8, k], v % 8) for v in range(k + 1, PANEL)}
                if k + 1 < PANEL:
                    ahead = row_of(col[g0 + (k + 1) // 8, k + 1], (k + 1) % 8)
                    d_next = ahead - (below[k + 1] * below[k + 1]) * inv
                    inv_next = 1.0 / d_next
                one = lane == c0 + k
                row = jnp.where(one, 1.0, row_of(w[gk], ks))
                for i in range(gk, per):
                    m = col[i, k] * inv
                    if i == gk:
                        m = jnp.where(sub > ks, m, 0.0)
                    for v in range(k + 1, PANEL):
                        if i >= g0 + v // 8:
                            col[i, v] = col[i, v] - m * below[v]
                    gone = one & (sub > ks) if i == gk else one
                    w[i] = jnp.where(gone, 0.0, w[i]) - m * row
                if k + 1 < PANEL:
                    d, inv = d_next, inv_next
        inside = (lane >= s0) & (lane < s0 + STRIP)
        scaled = []
        for i in range(per):
            scale = lax.rsqrt(pivot[i])
            v = w[i] * scale
            row = sub + (s0 + 8 * i)
            lower = jnp.where(lane < row, v, jnp.where(lane == row, scale, 0.0))
            write(per * t + i, jnp.where(lane >= row, v, 0.0), lower)
            scaled.append(jnp.where(inside, lower, v))
        if s0 + STRIP < NB:
            hi, lo = split(jnp.concatenate(scaled, axis=0))
            off = dot_t(jnp.concatenate([hi, hi, lo], axis=0), jnp.concatenate([hi, lo, hi], axis=0))
            for i in range(per * (t + 1), groups):
                a[i] = jnp.where(inside, 0.0, a[i]) - off[8 * i : 8 * i + 8, :]


def three(hi, lo, axis):
    return jnp.concatenate([hi, hi, lo], axis=axis)


def three_other(hi, lo, axis):
    return jnp.concatenate([hi, lo, hi], axis=axis)


def factor_kernel(n_quarter, n_layer, own_ref, far_ref, root_ref, info_ref, g, s, minv, r, uhi, ulo, thi, tlo, y):
    width = r.shape[1]
    nb = width // NB
    place, _ = packed_rows(width)
    blk, layer = lax.axis_index("blk"), lax.axis_index("fibre")
    side, quarter = blk % 2, blk // 2
    piece = own_ref.shape[0] // (n_quarter * n_layer)
    for mc, ref in enumerate((own_ref, far_ref)):
        held = side ^ mc
        for ns, ms in enumerate(distances(n_quarter, held != 0)):
            for nz, mz in enumerate(distances(n_layer, False)):
                to = ((held * n_quarter + (quarter ^ ms)) * n_layer + (layer ^ mz)) * piece
                at = (ns * n_layer + nz) * piece
                g[pl.ds(pl.multiple_of(to, 8), piece), :] = ref[at : at + piece, :]

    hw, q = NB // 2, NB // 4

    def block(i, j):
        if i != j:
            return g[place[i, j] : place[i, j] + NB, :]
        at = place[i, "top"]
        top = g[at : at + hw, :]
        at = place[i - i % 2, "corner"]
        corner = g[at : at + hw, :]
        mirror = jnp.concatenate([top, top], axis=0).T
        lane = lax.broadcasted_iota(jnp.int32, (hw, NB), 1)
        if i % 2 == 0:
            corner = jnp.concatenate([corner[:, hw:], corner[:, :hw]], axis=1)
        if i == 0:
            row = lax.broadcasted_iota(jnp.int32, (hw, NB), 0)
            top = jnp.where((lane < q) & (row >= q), mirror[:hw, :], top)
        return jnp.concatenate([top, jnp.where(lane < hw, mirror[hw:, :], corner)], axis=0)

    def span(i):
        return slice(i * NB, i * NB + NB)

    for b in range(width // q):
        at = place[0, "top"] + q + b
        y[:, b * q : (b + 1) * q] = jnp.broadcast_to(g[at : at + 1, 0:q], (8, q))
    s[span(0), span(0)] = block(0, 0)

    def inverse(i):
        return split(minv[span(i), :])

    def solve(i, c):
        mh, ml = inverse(i)
        sh, sl = split(s[span(i), c])
        u = jnp.dot(three(mh, ml, 1), three_other(sh, sl, 0), preferred_element_type=F32)
        r[span(i), c] = u
        uh, ul = split(u)
        uhi[span(i), c] = uh
        ulo[span(i), c] = ul
        return uh, ul

    def turn(i, b):
        th, tl = split(r[span(i), span(b)].T)
        thi[span(b), span(i)] = th
        tlo[span(b), span(i)] = tl

    def reduce(i, c, rows):
        up = slice(0, rows * NB)
        off = jnp.dot(
            three(thi[span(i), up], tlo[span(i), up], 1),
            three_other(uhi[up, c], ulo[up, c], 0),
            preferred_element_type=F32,
        )
        for b in range(c.start // NB, c.stop // NB):
            s[span(i), span(b)] = block(i, b) - off[:, b * NB - c.start : b * NB - c.start + NB]

    def rest_of(i):
        cuts = [slice(c, min(c + 2 * NB, width)) for c in range((i + 2) * NB, width, 2 * NB)]
        for c in cuts:
            solve(i, c)
            yield
        if i + 2 < nb:
            turn(i, i + 1)
            turn(i, i + 2)
            reduce(i + 2, span(i + 2), i + 1)
            yield
        for c in cuts:
            reduce(i + 1, c, i + 1)
            yield
        for b in range(i + 3, nb):
            turn(i, b)
        mh, ml = inverse(i)
        bh, bl = split(y[:, span(i)])
        yi = lax.dot_general(
            three(bh, bl, 1), three_other(mh, ml, 1), (((1,), (1,)), ((), ())), preferred_element_type=F32
        )
        y[:, span(i)] = yi
        yield
        if i + 1 < nb:
            c = slice((i + 1) * NB, width)
            yh, yl = split(yi)
            y[:, c] -= jnp.dot(
                three(yh, yl, 1), three_other(uhi[span(i), c], ulo[span(i), c], 0), preferred_element_type=F32
            )
            yield
        if i:
            r[span(i), 0 : i * NB] = jnp.zeros((NB, i * NB), F32)
            yield

    def begin():
        s[span(1), span(1)] = block(1, 1)
        yield
        for b in range(1, nb):
            s[span(0), span(b)] = block(0, b)
        yield

    other_work = begin()
    for i in range(nb):

        def read(u):
            return s[i * NB + 8 * u : i * NB + 8 * u + 8, span(i)]

        def write(u, upper, lower):
            at = slice(i * NB + 8 * u, i * NB + 8 * u + 8)
            r[at, span(i)] = upper
            minv[at, :] = lower

        factor_block(read, write, other_work)
        for _ in other_work:
            pass
        if i + 1 < nb:
            uh, ul = solve(i, span(i + 1))
            at = slice((i + 1) * NB, (i + 2) * NB)
            s[at, at] -= dot_t(three(uh, ul, 0), three_other(uh, ul, 0))
        other_work = rest_of(i)
    for _ in other_work:
        pass
    rows = root_ref.shape[0]
    root_ref[...] = r[pl.ds(pl.multiple_of(blk * rows, 8), rows), :]
    for b in range(nb):
        info_ref[b : b + 1, :] = y[0:1, span(b)]


def factor(own, far, n_quarter, n_layer, width, rows):
    whole = pl.BlockSpec(memory_space=pltpu.VMEM)
    nb = width // NB
    return pl.pallas_call(
        functools.partial(factor_kernel, n_quarter, n_layer),
        in_specs=[whole] * 2,
        out_specs=[whole] * 2,
        out_shape=[jax.ShapeDtypeStruct((rows, width), F32), jax.ShapeDtypeStruct((nb, NB), F32)],
        scratch_shapes=[
            pltpu.VMEM((2 * own.shape[0], NB), F32),
            pltpu.VMEM((width, width), F32),
            pltpu.VMEM((width, NB), F32),
            pltpu.VMEM((width, width), F32),
        ]
        + [pltpu.VMEM((width, width), BF16)] * 4
        + [pltpu.VMEM((8, width), F32)],
        compiler_params=vmem(28),
        name="factor",
    )(own, far)


def turns(n, odd):
    first = list(range(1, n))
    return first[::-1] if odd else first


def swap(x, axis, step):
    n_blk, n_fibre = lax.axis_size("blk"), lax.axis_size("fibre")
    pairs = []
    for f in range(n_fibre):
        for d in range(n_blk):
            if axis == "side":
                to = f, d ^ 1
            elif axis == "blk":
                to = f, d ^ 2 * turns(n_blk // 2, d % 2)[step]
            else:
                to = f ^ turns(n_fibre, 0)[step], d
            pairs.append((f * n_blk + d, to[0] * n_blk + to[1]))
    return lax.ppermute(x, ("fibre", "blk"), pairs)


def distances(n, odd):
    return [0] + [jnp.where(odd, o, e) for e, o in zip(turns(n, 0), turns(n, 1))]


def shares(parts, count, me, odd):
    rows = parts[0].shape[0] // count
    return [
        functools.reduce(lambda a, b: a + b, [lax.dynamic_slice_in_dim(x, (me ^ m) * rows, rows, 0) for x in parts])
        for m in distances(count, odd)
    ]


def trade(mine, axis):
    return [mine[0]] + [swap(x, axis, n) for n, x in enumerate(mine[1:])]


def gather(x, axis, count):
    return jnp.concatenate([x] + [swap(x, axis, n) for n in range(count - 1)], axis=0)


def local(readings, values, counts, prior_root, prior_info):
    width = readings.shape[1]
    n_blk, n_fibre = lax.axis_size("blk"), lax.axis_size("fibre")
    blk, fibre = lax.axis_index("blk"), lax.axis_index("fibre")
    n_quarter = n_blk // 2
    odd = blk % 2 != 0
    unit = 8 * n_blk * n_fibre
    sent = -(-packed_rows(width)[1] // unit) * unit

    keep, send = gram(readings, values, counts, prior_root, prior_info, sent)
    parts = [keep, swap(send, "side", 0)]
    parts = trade(shares(parts, n_quarter, blk // 2, odd), "blk")
    parts = trade(shares(parts, n_fibre, fibre, False), "fibre")
    own = functools.reduce(lambda x, y: x + y, parts)
    own = gather(gather(own, "fibre", n_fibre), "blk", n_quarter)
    far = swap(own, "side", 0)
    root, info = factor(own, far, n_quarter, n_fibre, width, width // n_blk)
    return root, info.reshape(width)


def solution(mesh):
    placed = (
        P(("fibre", "blk"), None),
        P(("fibre", "blk")),
        P(("fibre", "blk")),
        P(("fibre", "blk"), None),
        P(("fibre", "blk")),
    )
    return jax.shard_map(
        local, mesh=mesh, in_specs=placed, out_specs=(P("blk", None), P()), check_vma=False
    )
```
